256 devices in a mesh: lat: 32 (over z_hi, x, core), lev: 8 (over z_lo, y).
Axes of the slice: x: 4, y: 4, z: 8 (z_hi: 4, z_lo: 2; z = z_hi * 2 + z_lo), core: 2. Of those that a mesh axis runs over, the one named last changes fastest.
Arguments:
- velocity: float32 [2, 32, 256, 1152], P(None, 'lev', 'lat'), may hold values from -0.6 to 0.6
- potential_temp: float32 [32, 256, 1152], P('lev', 'lat'), may hold values from 0.5 to 1.5
- tracer: float32 [32, 256, 1152], P('lev', 'lat'), may hold values from 0.1 to 1
- thickness: float32 [32, 256, 1152], P('lev', 'lat'), may hold values from 0.5 to 1.5
- surface_height: float32 [256, 1152], P('lat'), may hold values from 0 to 1
- level_fractions: float32 [32], replicated, may hold values from 0.25 to 4
Outputs:
- remapped: float32 [4, 32, 256, 1152], P(None, 'lev', 'lat')
- new_thickness: float32 [32, 256, 1152], P('lev', 'lat')
- geopotential: float32 [32, 256, 1152], P('lev', 'lat')
The draws below stay inside these ranges and needn't reach their ends.
All inputs are finite; a program needn't handle non-finite values.
Results may differ from the reference program's by a relative error of at most 0.0003.
Values sent between devices are 32-bit elements; how exact they have to be, the bound alone decides.
A program may use at most 64 MiB of HBM per device.

```python
import math
import jax
import jax.numpy as jnp
from jax import lax

LON = 1152
SUBSTEPS = 4
LATS = 256
LEVELS = 32


def steps_of(key, dims, shards, low, largest):
    loudness, own = 1.0, jax.random.fold_in(key, 6)
    for dim, parts in shards:
        steps = jnp.exp(jax.random.uniform(jax.random.fold_in(own, dim), (parts,), jnp.float32, low / len(shards), largest / len(shards)))
        loudness = loudness * jnp.repeat(steps, dims[dim] // parts).reshape([-1 if axis == dim else 1 for axis in range(len(dims))])
    return loudness


def setup_inputs(seed: int = 0) -> dict:
    seeds = jax.random.split(jax.random.key(seed), 7)
    velocity = jnp.clip(jax.random.uniform(seeds[0], (2, LEVELS, LATS, LON), jnp.float32, -0.6, 0.6) * steps_of(seeds[0], (2, LEVELS, LATS, LON), ((1, 8), (2, 32)), -0.4, 0.0), -0.6, 0.6)
    potential_temp = jnp.clip(0.5 + 1.0 * jax.random.uniform(seeds[1], (LEVELS, LATS, LON), jnp.float32) ** steps_of(seeds[1], (LEVELS, LATS, LON), ((0, 8), (1, 32)), -0.2, 0.2), 0.5, 1.5)
    tracer = jnp.clip(jnp.exp(math.log(1.0) - 2.3025851 * jax.random.uniform(seeds[2], (LEVELS, LATS, LON), jnp.float32) ** steps_of(seeds[2], (LEVELS, LATS, LON), ((0, 8), (1, 32)), -0.2, 0.2)), 0.1, 1.0)
    thickness = jnp.clip(0.5 + 1.0 * jax.random.uniform(seeds[3], (LEVELS, LATS, LON), jnp.float32) ** steps_of(seeds[3], (LEVELS, LATS, LON), ((0, 8), (1, 32)), -0.2, 0.2), 0.5, 1.5)
    surface_height = jnp.clip(1.0 * jax.random.uniform(seeds[4], (LATS, LON), jnp.float32) ** steps_of(seeds[4], (LATS, LON), ((0, 32),), -0.2, 0.2), 0.0, 1.0)
    level_fractions = jnp.clip(jnp.exp(jax.random.uniform(seeds[5], (LEVELS,), jnp.float32, math.log(0.25), math.log(4.0))), 0.25, 4.0)
    return dict(velocity=velocity, potential_temp=potential_temp, tracer=tracer, thickness=thickness, surface_height=surface_height, level_fractions=level_fractions)


ADVECT = 0.3
PRESS = 0.15
ROTATION_RATE = 0.3
TOP_PRESSURE = 1.0


def zonal_slope(values):
    return (8.0 * (jnp.roll(values, -1, -1) - jnp.roll(values, 1, -1)) - (jnp.roll(values, -2, -1) - jnp.roll(values, 2, -1))) / 12.0


def polar_slope(padded):
    return (8.0 * (padded[..., 3:-1, :] - padded[..., 1:-3, :]) - (padded[..., 4:, :] - padded[..., :-4, :])) / 12.0


def coriolis(row_ids, latitude_strip_summation):
    angle = -0.5 * jnp.pi + (row_ids.astype(jnp.float32) + 0.5) * (jnp.pi / latitude_strip_summation)
    return (ROTATION_RATE * jnp.sin(angle))[:, None]


def substep(padded, turning):
    interior = padded[..., 2:-2, :]
    east_slope = zonal_slope(interior)
    north_slope = polar_slope(padded)
    eastward = interior[0]
    northward = interior[1]
    carried = ADVECT * (eastward * east_slope + northward * north_slope)
    new_east = eastward - carried[0] - PRESS * east_slope[4] + turning * northward
    new_north = northward - carried[1] - PRESS * north_slope[4] - turning * eastward
    new_temp = interior[2] - carried[2]
    new_tracer = interior[3] - carried[3]
    new_log = interior[4] - carried[4] - ADVECT * (east_slope[0] + north_slope[1])
    return jnp.stack([new_east, new_north, new_temp, new_tracer, new_log], 0)


def count_below(lower_edge, target_interfaces):
    levels = lower_edge.shape[0]
    block_size = 16 if levels % 16 == 0 else levels

    def add_block(number, running_count):
        slab_edges = lax.dynamic_slice_in_dim(lower_edge, number * block_size, block_size, 0)
        return running_count + jnp.sum((slab_edges[:, None] < target_interfaces[None]).astype(jnp.int32), axis=0, dtype=jnp.int32)

    return lax.fori_loop(0, levels // block_size, add_block, jnp.zeros(target_interfaces.shape, jnp.int32))


def remap(gridded_quantities, level_fractions):
    values = gridded_quantities[:4]
    layer_thick = gridded_quantities[4]
    levels = layer_thick.shape[0]
    trailing = (1,) * (layer_thick.ndim - 1)
    lower_edge = jnp.cumsum(layer_thick, axis=0)
    upper_edge = lower_edge - layer_thick
    bottom_pressure = lower_edge[-1]
    portion = level_fractions / jnp.sum(level_fractions)
    bounds = jnp.concatenate([jnp.zeros((1,), jnp.float32), jnp.cumsum(portion)])
    target_interfaces = bottom_pressure[None] * bounds.reshape((levels + 1,) + trailing)
    position = jnp.minimum(count_below(lower_edge, target_interfaces), levels - 1)
    weighted = values * layer_thick[None]
    before = jnp.cumsum(weighted, axis=1) - weighted
    indices = jnp.broadcast_to(position[None], (4,) + position.shape)
    start_edge = jnp.take_along_axis(upper_edge, position, axis=0)
    integral = jnp.take_along_axis(before, indices, axis=1) + (target_interfaces - start_edge)[None] * jnp.take_along_axis(values, indices, axis=1)
    new_thickness = bottom_pressure[None] * portion.reshape((levels,) + trailing)
    remapped = (integral[:, 1:] - integral[:, :-1]) / new_thickness[None]
    return remapped, new_thickness, target_interfaces


def vertical_stack_heights(thermal_state_field, target_interfaces, terrain_floor):
    atmospheric_stress_field = TOP_PRESSURE + target_interfaces
    sheet_thickness_delta = thermal_state_field * jnp.log(atmospheric_stress_field[1:] / atmospheric_stress_field[:-1])
    return terrain_floor[None] + jnp.flip(jnp.cumsum(jnp.flip(sheet_thickness_delta, 0), 0), 0)


def reference(velocity, potential_temp, tracer, thickness, surface_height, level_fractions):
    gridded_quantities = jnp.concatenate([velocity, potential_temp[None], tracer[None], jnp.log(thickness)[None]], 0)
    latitude_strip_summation = gridded_quantities.shape[2]
    turning = coriolis(jnp.arange(latitude_strip_summation, dtype=jnp.int32), latitude_strip_summation)

    def advance(level_fields):
        for repeat in range(SUBSTEPS):
            padded = jnp.pad(level_fields, ((0, 0), (2, 2), (0, 0)))
            level_fields = substep(padded, turning)
        return jnp.concatenate([level_fields[:4], jnp.exp(level_fields[4:])], 0)

    advanced = lax.map(advance, jnp.transpose(gridded_quantities, (1, 0, 2, 3)))
    by_row = jnp.transpose(advanced, (2, 1, 0, 3))

    def column_row(inputs):
        row_fields, terrain_floor = inputs
        remapped, new_thickness, target_interfaces = remap(row_fields, level_fractions)
        heights = vertical_stack_heights(remapped[2], target_interfaces, terrain_floor)
        return remapped, new_thickness, heights

    remapped, new_thickness, heights = lax.map(column_row, (by_row, surface_height))
    return jnp.transpose(remapped, (1, 2, 0, 3)), jnp.transpose(new_thickness, (1, 0, 2)), jnp.transpose(heights, (1, 0, 2))
```

```python
import functools
import math

import jax
import jax.numpy as jnp
from jax import lax
from jax.experimental import pallas as pl
from jax.experimental.pallas import tpu as pltpu
from jax.sharding import PartitionSpec as P

MESH = pl.DeviceIdType.MESH
SUBSTEPS = 4
ADVECT = 0.3 / 12.0
PRESS = 0.15 / 12.0
ROTATION_RATE = 0.3
TOP_PRESSURE = 1.0

ROWS = 8
LON = 1152
CHUNKS = 3
TILES = 3
WIDE = 128 * TILES
SENT = 2 * WIDE + 256
BACK = 3 * WIDE
PEERS = 8


def kernel(
    lat_size,
    vel_ref, temp_ref, tracer_ref, thick_ref, surf_ref, frac_ref,
    out_ref, out_thick_ref, out_geo_ref,
    band, uv_a, pq_a, s_a, uv_b, pq_b, s_b, turn, bound, share, surf,
    fwd, got, ret, back, result,
    local_sem, halo_send, halo_recv, fwd_send, fwd_recv, ret_send, ret_recv, out_sem,
):
    lat, lev = lax.axis_index("lat"), lax.axis_index("lev")
    north = lax.rem(lat + lat_size - 1, lat_size)
    south = lax.rem(lat + 1, lat_size)

    def peer(step):
        return lax.rem(lev + 1 + step, PEERS)

    parts = ((vel_ref, 0, 64), (temp_ref, 64, 32), (tracer_ref, 96, 32), (thick_ref, 128, 32))
    own = [
        pltpu.make_async_copy(ref, band.at[1, pl.ds(at, size)], local_sem.at[n])
        for n, (ref, at, size) in enumerate(parts)
    ]
    own.append(pltpu.make_async_copy(surf_ref, surf, local_sem.at[4]))
    for copy in own:
        copy.start()

    barrier = pltpu.get_barrier_semaphore()
    for row in (north, south):
        pl.semaphore_signal(barrier, inc=1, device_id=(row, lev), device_id_type=MESH)
    for step in range(PEERS - 1):
        pl.semaphore_signal(barrier, inc=1, device_id=(lat, peer(step)), device_id_type=MESH)
    pl.semaphore_wait(barrier, PEERS + 1)

    halo = [
        pltpu.make_async_remote_copy(
            src_ref=ref,
            dst_ref=band.at[where, pl.ds(at, size)],
            send_sem=halo_send.at[way, n],
            recv_sem=halo_recv.at[way, n],
            device_id=(row, lev),
            device_id_type=MESH,
        )
        for way, (row, where) in enumerate(((south, 0), (north, 2)))
        for n, (ref, at, size) in enumerate(parts)
    ]
    for copy in halo:
        copy.start()

    total = jnp.float32(0.0)
    for k in range(4 * PEERS):
        total = total + frac_ref[k]
        share[k, :] = jnp.full((128,), frac_ref[k], jnp.float32)
        bound[k, :] = jnp.full((128,), total, jnp.float32)
    share[...] = share[...] / total
    bound[...] = bound[...] / total

    sub = lax.broadcasted_iota(jnp.int32, (8, 128), 0)
    low = lax.broadcasted_iota(jnp.int32, (8, LON), 0) < 4
    row_of = lax.broadcasted_iota(jnp.int32, (3 * ROWS, 8, 128), 0) + (lat - 1) * ROWS
    angle = -0.5 * math.pi + (row_of.astype(jnp.float32) + 0.5) * (math.pi / (lat_size * ROWS))
    sign = jnp.where(lax.broadcasted_iota(jnp.int32, (3 * ROWS, 8, 128), 1) < 4, ROTATION_RATE, -ROTATION_RATE)
    turn[...] = sign * jnp.sin(angle)

    def inside(j):
        row = (lat - 1) * ROWS + j
        return jnp.where((row >= 0) & (row < lat_size * ROWS), 1.0, 0.0).astype(jnp.float32)

    def transposed(xs):
        for d in (4, 2, 1):
            ys = list(xs)
            for i in range(8):
                if not i & d:
                    ys[i] = jnp.where(sub & d == 0, xs[i], pltpu.roll(xs[i + d], d, 0))
                    ys[i + d] = jnp.where(sub & d == 0, pltpu.roll(xs[i], 8 - d, 0), xs[i + d])
            xs = ys
        return xs

    def unpack(b):
        keep = inside(b * ROWS)

        def body(t, carry):
            lanes = pl.ds(pl.multiple_of(t * 128, 128), 128)
            for dst, at in ((uv_a, 0), (pq_a, 64)):
                xs = [band[b, at + 8 * i : at + 8 * i + 8, lanes] * keep for i in range(8)]
                for r, x in enumerate(transposed(xs)):
                    dst[b * ROWS + r, :, lanes] = x
            xs = [jnp.log(band[b, 128 + 8 * i : 136 + 8 * i, lanes]) * keep for i in range(4)]
            for r, x in enumerate(transposed(xs + xs)):
                s_a[b * ROWS + r, :, lanes] = x
            return carry

        lax.fori_loop(0, LON // 128, body, 0)

    def east(a):
        return 8.0 * (pltpu.roll(a, LON - 1, 1) - pltpu.roll(a, 1, 1)) - (
            pltpu.roll(a, LON - 2, 1) - pltpu.roll(a, 2, 1)
        )

    def up(ref, j):
        return 8.0 * (ref[j + 1] - ref[j - 1]) - (ref[j + 2] - ref[j - 2])

    def advance(state, j):
        uv_ref, pq_ref, s_ref = state
        uv, pq, s = uv_ref[j], pq_ref[j], s_ref[j]
        turned = pltpu.roll(uv, 4, 0)
        eastward = jnp.where(low, uv, turned) * ADVECT
        northward = jnp.where(low, turned, uv) * ADVECT
        new_pq = pq - eastward * east(pq) - northward * up(pq_ref, j)
        s_east, s_up = east(s), up(s_ref, j)
        uv_east, uv_up = east(uv), up(uv_ref, j)
        spin = jnp.concatenate([turn[j]] * (LON // 128), axis=1)
        new_uv = uv - eastward * uv_east - northward * uv_up - PRESS * jnp.where(low, s_east, s_up) + spin * turned
        spread = jnp.where(low, uv_east, uv_up)
        new_s = s - eastward * s_east - northward * s_up - ADVECT * (spread + pltpu.roll(spread, 4, 0))
        return new_uv, new_pq, new_s

    def substep(src, dst, first, last):
        def body(j, carry):
            keep = inside(j)
            new_uv, new_pq, new_s = advance(src, j)
            dst[0][j] = new_uv * keep
            dst[1][j] = new_pq
            dst[2][j] = new_s * keep
            return carry

        lax.fori_loop(first, last, body, 0)

    a, b = (uv_a, pq_a, s_a), (uv_b, pq_b, s_b)
    for copy in own:
        copy.wait()
    unpack(1)
    substep(a, b, 10, 14)
    for copy in halo[:4]:
        copy.wait()
    unpack(0)
    substep(a, b, 2, 10)
    for copy in halo[4:]:
        copy.wait()
    unpack(2)
    substep(a, b, 14, 22)
    substep(b, a, 4, 20)
    substep(a, b, 6, 18)

    def message(r, put):
        new_uv, new_pq, new_s = advance(b, ROWS + r)
        for c in range(CHUNKS):
            at = c * WIDE
            put(c, slice(0, WIDE), new_uv[:, at : at + WIDE])
            put(c, slice(WIDE, 2 * WIDE), new_pq[:, at : at + WIDE])
            s0, s1, s2 = (new_s[:, at + 128 * t : at + 128 * (t + 1)] for t in range(TILES))
            put(c, slice(2 * WIDE, 2 * WIDE + 128), jnp.where(sub < 4, s0, s2))
            put(c, slice(2 * WIDE + 128, SENT), s1)

    def fwd_copy(c, step):
        return pltpu.make_async_remote_copy(
            src_ref=fwd.at[c, step],
            dst_ref=got.at[c, lev],
            send_sem=fwd_send.at[c, step],
            recv_sem=fwd_recv.at[c, step],
            device_id=(lat, peer(step)),
            device_id_type=MESH,
        )

    def last_row(step, carry):
        def put(c, lanes, value):
            fwd[c, step, :, lanes] = value

        message(peer(step), put)
        fwd_copy(0, step).start()
        return carry

    lax.fori_loop(0, PEERS - 1, last_row, 0)
    for c in range(1, CHUNKS):
        lax.fori_loop(0, PEERS - 1, lambda k, z, c=c: (fwd_copy(c, k).start(), z)[1], 0)

    def put_own(c, lanes, value):
        got[c, lev, :, lanes] = value

    message(lev, put_own)

    def ret_copy(c, step):
        return pltpu.make_async_remote_copy(
            src_ref=ret.at[c, peer(step)],
            dst_ref=back.at[c, lev],
            send_sem=ret_send.at[c, step],
            recv_sem=ret_recv.at[c, step],
            device_id=(lat, peer(step)),
            device_id_type=MESH,
        )

    small = sub < 4

    def flip(x):
        return pltpu.roll(x, 4, 0)

    def running(values):
        out, carry = [], None
        for v in values:
            for d in (1, 2, 4):
                v = v + jnp.where(sub >= d, pltpu.roll(v, d, 0), 0.0)
            if carry is not None:
                v = v + carry
            out.append(v)
            carry = v[7:8]
        return out

    def previous(values):
        out, carry = [], jnp.zeros((1, 128), jnp.float32)
        for v in values:
            out.append(jnp.where(sub == 0, carry, pltpu.roll(v, 1, 0)))
            carry = v[7:8]
        return out

    def gather(x, index):
        return jnp.take_along_axis(x, index, axis=0, mode="promise_in_bounds")

    def tile(c, t):
        at = pl.multiple_of(t * 128, 128)

        def split(start):
            xs = [got[c, p, :, pl.ds(start + at, 128)] for p in range(PEERS)]
            first = [jnp.where(small, xs[2 * i], flip(xs[2 * i + 1])) for i in range(4)]
            second = [jnp.where(small, flip(xs[2 * i]), xs[2 * i + 1]) for i in range(4)]
            return first, second

        u, v = split(0)
        temp, tracer = split(WIDE)
        high = t == 2
        s_at = pl.multiple_of(2 * WIDE + jnp.where(high, 0, t) * 128, 128)
        xs = [got[c, p, :, pl.ds(s_at, 128)] for p in range(PEERS)]
        layer = []
        for i in range(4):
            lower_half = jnp.where(small, xs[2 * i], flip(xs[2 * i + 1]))
            upper_half = jnp.where(small, flip(xs[2 * i]), xs[2 * i + 1])
            layer.append(jnp.exp(jnp.where(high, upper_half, lower_half)))
        lower = running(layer)
        upper = [x - y for x, y in zip(lower, layer)]
        bottom = lower[3][7:8]
        fields = (u, v, temp, tracer)
        before = []
        for f in fields:
            weighted = [x * y for x, y in zip(f, layer)]
            before.append([x - y for x, y in zip(running(weighted), weighted)])
        target = [bottom * bound[8 * i : 8 * i + 8, :] for i in range(4)]
        integral = [[] for _ in fields]
        ends = [lower[m][7:8] for m in range(3)]
        mids = [jnp.broadcast_to(lower[m][3:4], (8, 128)) for m in range(4)]
        for i in range(4):
            goal = target[i]
            past = [goal > e for e in ends]

            def pick(q):
                return jnp.where(past[2], q[3], jnp.where(past[1], q[2], jnp.where(past[0], q[1], q[0])))

            pos = jnp.where(pick(mids) < goal, 4, 0)
            pos = pos + jnp.where(pick([gather(x, pos + 1) for x in lower]) < goal, 2, 0)
            pos = pos + jnp.where(pick([gather(x, pos) for x in lower]) < goal, 1, 0)

            def here(q):
                return pick([gather(x, pos) for x in q])

            depth = goal - here(upper)
            for n, f in enumerate(fields):
                integral[n].append(here(before[n]) + depth * here(f))
        new_thick = [bottom * share[8 * i : 8 * i + 8, :] for i in range(4)]
        inverse = [1.0 / x for x in new_thick]
        remapped = [[(x - y) * z for x, y, z in zip(g, previous(g), inverse)] for g in integral]
        rise = [
            r * jnp.log((TOP_PRESSURE + x) / (TOP_PRESSURE + y))
            for r, x, y in zip(remapped[2], target, previous(target))
        ]
        geo = [None] * 4
        ground = surf[:, pl.ds(pl.multiple_of(c * WIDE + t * 128, 128), 128)]
        carry = jnp.sum(jnp.where(sub == lev, ground, 0.0), axis=0, keepdims=True)
        for i in (3, 2, 1, 0):
            x = rise[i]
            for d in (1, 2, 4):
                x = x + jnp.where(sub < 8 - d, pltpu.roll(x, 8 - d, 0), 0.0)
            geo[i] = x + carry
            carry = geo[i][0:1]
        for start, (one, two) in (
            (0, (remapped[0], remapped[1])),
            (WIDE, (remapped[2], remapped[3])),
            (2 * WIDE, (geo, new_thick)),
        ):
            for i in range(4):
                ret[c, 2 * i, :, pl.ds(start + at, 128)] = jnp.where(small, one[i], flip(two[i]))
                ret[c, 2 * i + 1, :, pl.ds(start + at, 128)] = jnp.where(small, flip(one[i]), two[i])

    def chunk(c, carry):
        lax.fori_loop(0, PEERS - 1, lambda k, z: (fwd_copy(c, k).wait_recv(), z)[1], 0)
        lax.fori_loop(0, TILES, lambda t, z: (tile(c, t), z)[1], 0)
        lax.fori_loop(0, PEERS - 1, lambda k, z: (ret_copy(c, k).start(), z)[1], 0)
        return carry

    lax.fori_loop(0, CHUNKS, chunk, 0)

    def deliver(c, carry):
        lax.fori_loop(0, PEERS - 1, lambda k, z: (ret_copy(c, k).wait_recv(), z)[1], 0)
        lax.fori_loop(0, PEERS - 1, lambda k, z: (ret_copy(c, k).wait_send(), z)[1], 0)
        back[c, lev] = ret[c, lev]

        def body(t, carry):
            at = pl.multiple_of(t * 128, 128)
            lanes = pl.ds(pl.multiple_of(c * WIDE + t * 128, 128), 128)
            for n in range(3):
                xs = [back[c, r, :, pl.ds(n * WIDE + at, 128)] for r in range(ROWS)]
                for i, x in enumerate(transposed(xs)):
                    result[64 * n + 8 * i : 64 * n + 8 * i + 8, lanes] = x
            return carry

        lax.fori_loop(0, TILES, body, 0)
        return carry

    lax.fori_loop(0, CHUNKS, deliver, 0)

    outs = [
        pltpu.make_async_copy(result.at[pl.ds(at, size)], ref, out_sem.at[n])
        for n, (ref, at, size) in enumerate(((out_ref, 0, 128), (out_geo_ref, 128, 32), (out_thick_ref, 160, 32)))
    ]
    for copy in outs:
        copy.start()

    def sent(n, carry):
        c, step = n // (PEERS - 1), lax.rem(n, PEERS - 1)
        fwd_copy(c, step).wait_send()
        return carry

    lax.fori_loop(0, CHUNKS * (PEERS - 1), sent, 0)
    for copy in outs:
        copy.wait()


def shards(lat_size, velocity, potential_temp, tracer, thickness, surface_height, level_fractions):
    anywhere = pl.BlockSpec(memory_space=pl.ANY)
    f32 = jnp.float32
    state = [pltpu.VMEM((3 * ROWS, 8, LON), f32)] * 6
    remapped, new_thickness, geopotential = pl.pallas_call(
        functools.partial(kernel, lat_size),
        out_shape=(
            jax.ShapeDtypeStruct((128, LON), f32),
            jax.ShapeDtypeStruct((32, LON), f32),
            jax.ShapeDtypeStruct((32, LON), f32),
        ),
        in_specs=[anywhere] * 5 + [pl.BlockSpec(memory_space=pltpu.SMEM)],
        out_specs=(anywhere,) * 3,
        scratch_shapes=[
            pltpu.VMEM((3, 160, LON), f32),
            *state,
            pltpu.VMEM((3 * ROWS, 8, 128), f32),
            pltpu.VMEM((32, 128), f32),
            pltpu.VMEM((32, 128), f32),
            pltpu.VMEM((ROWS, LON), f32),
            pltpu.VMEM((CHUNKS, PEERS - 1, 8, SENT), f32),
            pltpu.VMEM((CHUNKS, PEERS, 8, SENT), f32),
            pltpu.VMEM((CHUNKS, PEERS, 8, BACK), f32),
            pltpu.VMEM((CHUNKS, PEERS, 8, BACK), f32),
            pltpu.VMEM((192, LON), f32),
            pltpu.SemaphoreType.DMA((5,)),
            pltpu.SemaphoreType.DMA((2, 4)),
            pltpu.SemaphoreType.DMA((2, 4)),
            pltpu.SemaphoreType.DMA((CHUNKS, PEERS - 1)),
            pltpu.SemaphoreType.DMA((CHUNKS, PEERS - 1)),
            pltpu.SemaphoreType.DMA((CHUNKS, PEERS - 1)),
            pltpu.SemaphoreType.DMA((CHUNKS, PEERS - 1)),
            pltpu.SemaphoreType.DMA((3,)),
        ],
        compiler_params=pltpu.CompilerParams(
            collective_id=0, has_side_effects=True, vmem_limit_bytes=40 * 2**20
        ),
        cost_estimate=pl.CostEstimate(flops=10**8, bytes_accessed=2 * 10**6, transcendentals=10**6),
    )(
        velocity.reshape(64, LON),
        potential_temp.reshape(32, LON),
        tracer.reshape(32, LON),
        thickness.reshape(32, LON),
        surface_height,
        level_fractions,
    )
    return (
        remapped.reshape(4, 4, ROWS, LON),
        new_thickness.reshape(4, ROWS, LON),
        geopotential.reshape(4, ROWS, LON),
    )


def solution(mesh):
    return jax.shard_map(
        functools.partial(shards, mesh.shape["lat"]),
        mesh=mesh,
        in_specs=(
            P(None, "lev", "lat", None),
            P("lev", "lat", None),
            P("lev", "lat", None),
            P("lev", "lat", None),
            P("lat", None),
            P(),
        ),
        out_specs=(P(None, "lev", "lat", None), P("lev", "lat", None), P("lev", "lat", None)),
        check_vma=False,
    )
```

```python
import functools
import math

import jax
import jax.numpy as jnp
from jax import lax
from jax.experimental import pallas as pl
from jax.experimental.pallas import tpu as pltpu
from jax.sharding import PartitionSpec as P

MESH = pl.DeviceIdType.MESH
SUBSTEPS = 4
ADVECT = 0.3 / 12.0
PRESS = 0.15 / 12.0
ROTATION_RATE = 0.3
TOP_PRESSURE = 1.0

ROWS = 8
LON = 1152
TILES = 9
ROW = 2 * LON + 640
PIECE = 384
PEERS = 8
RING = 8


def kernel(
    lat_size,
    vel_ref, temp_ref, tracer_ref, thick_ref, surf_ref, frac_ref,
    out_ref, out_thick_ref, out_geo_ref,
    frac, band, rows, s_0, uv_1, pq_1, s_1, uv_2, pq_2, s_2, uv_3, pq_3, s_3, turn, bound, share, surf,
    relay, fwd, got, ret, back, result,
    local_sem, halo_send, halo_recv, relay_send, relay_recv, fwd_send, fwd_recv, ret_send, ret_recv, out_sem,
):
    lat, lev = lax.axis_index("lat"), lax.axis_index("lev")
    relayed = lat_size % RING == 0 and lat_size > RING

    def band_at(offset):
        return lax.rem(lat + offset + lat_size, lat_size)

    def lane(t):
        return slice(128 * t, 128 * t + 128)

    parts = ((vel_ref, 0, 64), (temp_ref, 64, 32), (tracer_ref, 96, 32), (thick_ref, 128, 32))
    own = [
        pltpu.make_async_copy(ref, band.at[pl.ds(at, size)], local_sem.at[n])
        for n, (ref, at, size) in enumerate(parts)
    ]
    later = [
        pltpu.make_async_copy(surf_ref, surf, local_sem.at[4]),
        pltpu.make_async_copy(frac_ref, frac, local_sem.at[5]),
    ]
    for copy in own + later:
        copy.start()

    has_north, has_south = lat > 0, lat < lat_size - 1
    before_step = lax.rem(lat, RING) == RING - 1
    after_step = lax.rem(lat, RING) == 0
    beside = band_at(jnp.where(before_step, 1 - RING, RING - 1))
    ahead, behind = lat + RING < lat_size, lat >= RING
    relays_south = after_step & ahead
    relays_north = before_step & behind

    barrier = pltpu.get_barrier_semaphore()

    def greet(row):
        pl.semaphore_signal(barrier, inc=1, device_id=(row, lev), device_id_type=MESH)

    def peer(step):
        return lax.rem(lev + 1 + step, PEERS)

    pl.when(has_north)(lambda: greet(band_at(-1)))
    pl.when(has_south)(lambda: greet(band_at(1)))
    for step in range(PEERS - 1):
        pl.semaphore_signal(barrier, inc=1, device_id=(lat, peer(step)), device_id_type=MESH)
    guests = PEERS - 1 + jnp.where(has_north, 1, 0) + jnp.where(has_south, 1, 0)
    if relayed:

        @pl.when(before_step | after_step)
        def _():
            greet(beside)
            pl.when(ahead)(lambda: greet(band_at(RING)))
            pl.when(behind)(lambda: greet(band_at(-RING)))

        more = 1 + jnp.where(ahead, 1, 0) + jnp.where(behind, 1, 0)
        guests = guests + jnp.where(before_step | after_step, more, 0)

    sub = lax.broadcasted_iota(jnp.int32, (8, 128), 0)
    lanes_in = lax.broadcasted_iota(jnp.int32, (8, 128), 1)
    small = sub < 4

    def flip(x):
        return pltpu.roll(x, 4, 0)

    def transposed(xs):
        for d in (4, 2, 1):
            ys = list(xs)
            for i in range(8):
                if not i & d:
                    ys[i] = jnp.where(sub & d == 0, xs[i], pltpu.roll(xs[i + d], d, 0))
                    ys[i + d] = jnp.where(sub & d == 0, pltpu.roll(xs[i], 8 - d, 0), xs[i + d])
            xs = ys
        return xs

    for copy in own:
        copy.wait()

    def unpack(t, carry):
        at = pl.multiple_of(t * 128, 128)
        for start, n in ((0, 0), (LON, 64)):
            xs = [band[n + 8 * i : n + 8 * i + 8, pl.ds(at, 128)] for i in range(8)]
            for r, x in enumerate(transposed(xs)):
                rows[ROWS + r, :, pl.ds(start + at, 128)] = x
        xs = [jnp.log(band[128 + 8 * i : 136 + 8 * i, pl.ds(at, 128)]) for i in range(4)]
        for r, x in enumerate(transposed(xs + xs)):
            s_0[ROWS + r, :, pl.ds(at, 128)] = x
        return carry

    lax.fori_loop(0, TILES, unpack, 0)

    def fold(r, carry):
        j = ROWS + r
        for t in range(4):
            x = jnp.where(small, s_0[j, :, lane(t)], s_0[j, :, lane(t + 5)])
            rows[j, :, 2 * LON + 128 * t : 2 * LON + 128 * (t + 1)] = x
        rows[j, :, 2 * LON + 512 :] = s_0[j, :, lane(4)]
        return carry

    lax.fori_loop(0, ROWS, fold, 0)

    pl.semaphore_wait(barrier, guests)

    def remote(src, dst, send, recv, to):
        return pltpu.make_async_remote_copy(
            src_ref=src, dst_ref=dst, send_sem=send, recv_sem=recv, device_id=to, device_id_type=MESH
        )

    def to_south(h, src=None, row=None, send=None):
        return remote(
            rows.at[2 * ROWS - h] if src is None else src,
            rows.at[ROWS - h],
            halo_send.at[0, h - 1] if send is None else send,
            halo_recv.at[0, h - 1],
            (band_at(1) if row is None else row, lev),
        )

    def to_north(h, src=None, row=None, send=None):
        return remote(
            rows.at[ROWS - 1 + h] if src is None else src,
            rows.at[2 * ROWS - 1 + h],
            halo_send.at[1, h - 1] if send is None else send,
            halo_recv.at[1, h - 1],
            (band_at(-1) if row is None else row, lev),
        )

    def to_relay(way, h):
        n = h // 2 - 1
        src = rows.at[2 * ROWS - h] if way == 0 else rows.at[ROWS - 1 + h]
        return remote(src, relay.at[n], halo_send.at[way, h - 1], relay_recv.at[n], (beside, lev))

    for h in range(1, ROWS + 1):
        if relayed and h % 2 == 0:
            pl.when(has_south & before_step)(lambda h=h: to_relay(0, h).start())
            pl.when(has_south & jnp.logical_not(before_step))(lambda h=h: to_south(h).start())
            pl.when(has_north & after_step)(lambda h=h: to_relay(1, h).start())
            pl.when(has_north & jnp.logical_not(after_step))(lambda h=h: to_north(h).start())
        else:
            pl.when(has_south)(lambda h=h: to_south(h).start())
            pl.when(has_north)(lambda h=h: to_north(h).start())

    def forward_south(h):
        return to_south(h, relay.at[h // 2 - 1], band_at(RING), relay_send.at[h // 2 - 1])

    def forward_north(h):
        return to_north(h, relay.at[h // 2 - 1], band_at(-RING), relay_send.at[h // 2 - 1])

    def pass_on(h):
        @pl.when(relays_south)
        def _():
            to_relay(0, h).wait_recv()
            forward_south(h).start()

        @pl.when(relays_north)
        def _():
            to_relay(1, h).wait_recv()
            forward_north(h).start()

    for copy in later:
        copy.wait()
    total = jnp.float32(0.0)
    for k in range(4 * PEERS):
        total = total + frac[k]
        share[k, :] = jnp.full((128,), frac[k], jnp.float32)
        bound[k, :] = jnp.full((128,), total, jnp.float32)
    share[...] = share[...] / total
    bound[...] = bound[...] / total
    row_of = lax.broadcasted_iota(jnp.int32, (3 * ROWS, 8, 128), 0) + (lat - 1) * ROWS
    angle = -0.5 * math.pi + (row_of.astype(jnp.float32) + 0.5) * (math.pi / (lat_size * ROWS))
    sign = jnp.where(lax.broadcasted_iota(jnp.int32, (3 * ROWS, 8, 128), 1) < 4, ROTATION_RATE, -ROTATION_RATE)
    turn[...] = sign * jnp.sin(angle)

    def inside(j):
        row = (lat - 1) * ROWS + j
        return jnp.where((row >= 0) & (row < lat_size * ROWS), 1.0, 0.0).astype(jnp.float32)

    def advance(state, js, emits):
        (uv_ref, _), (pq_ref, pq_at), (s_ref, _) = state
        fields = ((uv_ref, 0), (pq_ref, pq_at), (s_ref, 0))

        def line(j, emit):
            spin = turn[j]

            def load(n, row, t):
                ref, at = fields[n]
                return ref[row, :, at + 128 * t : at + 128 * (t + 1)]

            here, rolled = {}, {}

            def value(n, t):
                if (n, t) not in here:
                    here[n, t] = load(n, j, t)
                return here[n, t]

            def roll(n, t, k):
                t = t % TILES
                if (n, t, k) not in rolled:
                    rolled[n, t, k] = pltpu.roll(value(n, t), k, 1)
                return rolled[n, t, k]

            def east(n, t):
                one = jnp.where(lanes_in < 127, roll(n, t, 127), roll(n, t + 1, 127)) - jnp.where(
                    lanes_in < 1, roll(n, t - 1, 1), roll(n, t, 1)
                )
                two = jnp.where(lanes_in < 126, roll(n, t, 126), roll(n, t + 1, 126)) - jnp.where(
                    lanes_in < 2, roll(n, t - 1, 2), roll(n, t, 2)
                )
                return 8.0 * one - two

            def up(n, t):
                return 8.0 * (load(n, j + 1, t) - load(n, j - 1, t)) - (load(n, j + 2, t) - load(n, j - 2, t))

            def step(t):
                uv, pq, s = (value(n, t) for n in range(3))
                turned = flip(uv)
                eastward = jnp.where(small, uv, turned) * ADVECT
                northward = jnp.where(small, turned, uv) * ADVECT
                uv_east, uv_up = east(0, t), up(0, t)
                s_east, s_up = east(2, t), up(2, t)
                new_pq = pq - eastward * east(1, t) - northward * up(1, t)
                push = PRESS * jnp.where(small, s_east, s_up)
                new_uv = uv - eastward * uv_east - northward * uv_up - push + spin * turned
                spread = jnp.where(small, uv_east, uv_up)
                new_s = s - eastward * s_east - northward * s_up - ADVECT * (spread + flip(spread))
                emit(t, new_uv, new_pq, new_s)

            return step

        steps = [line(j, emit) for j, emit in zip(js, emits)]
        for t in range(TILES):
            for step in steps:
                step(t)

    states = (
        ((rows, 0), (rows, LON), (s_0, 0)),
        ((uv_1, 0), (pq_1, 0), (s_1, 0)),
        ((uv_2, 0), (pq_2, 0), (s_2, 0)),
        ((uv_3, 0), (pq_3, 0), (s_3, 0)),
    )

    def substep(n, *js):
        dst = states[n]

        def into(j):
            keep = inside(j)

            def emit(t, new_uv, new_pq, new_s):
                dst[0][0][j, :, lane(t)] = new_uv * keep
                dst[1][0][j, :, lane(t)] = new_pq
                dst[2][0][j, :, lane(t)] = new_s * keep

            return emit

        advance(states[n - 1], js, [into(j) for j in js])

    def receive(way, h):
        j = ROWS - h if way == 0 else 2 * ROWS - 1 + h
        there = has_north if way == 0 else has_south
        pl.when(there)(lambda: (to_south(h) if way == 0 else to_north(h)).wait_recv())

        @pl.when(jnp.logical_not(there))
        def _():
            rows[j] = jnp.zeros((8, ROW), jnp.float32)

        for t in range(5):
            x = rows[j, :, 2 * LON + 128 * t : 2 * LON + 128 * (t + 1)]
            y = flip(x)
            s_0[j, :, lane(t)] = jnp.where(small, x, y)
            if t < 4:
                s_0[j, :, lane(t + 5)] = jnp.where(small, y, x)

    def fwd_copy(r, step):
        t = lax.rem(peer(step) - r + PEERS, PEERS)
        return remote(
            fwd.at[r, t], got.at[r, lev], fwd_send.at[r, step], fwd_recv.at[r, step], (lat, peer(step))
        )

    def extra_copy(r):
        step = lax.rem(r - lev - 1 + 2 * PEERS, PEERS)
        return remote(fwd.at[r, 8], got.at[8, lev], fwd_send.at[8, step], fwd_recv.at[8, step], (lat, r))

    def release(*rs):
        def into(r):
            def emit(t, new_uv, new_pq, new_s):
                fwd[r, t, :, lane(0)] = new_uv
                fwd[r, t, :, lane(1)] = new_pq
                fwd[r, t, :, lane(2)] = new_s

            return emit

        advance(states[3], [ROWS + r for r in rs], [into(r) for r in rs])
        for r in rs:
            lax.fori_loop(0, PEERS - 1, lambda k, z, r=r: (fwd_copy(r, k).start(), z)[1], 0)
            pl.when(r != lev)(lambda r=r: extra_copy(r).start())
            got[r, lev] = fwd[r, lax.rem(lev - r + PEERS, PEERS)]

            @pl.when(r == lev)
            def _(r=r):
                got[8, lev] = fwd[r, 8]

    def ret_copy(u, row, t, step):
        return remote(
            ret.at[u, peer(step)], back.at[t, row], ret_send.at[u, step], ret_recv.at[u, step], (lat, peer(step))
        )

    def running(values):
        out, carry = [], None
        for v in values:
            for d in (1, 2, 4):
                v = v + jnp.where(sub >= d, pltpu.roll(v, d, 0), 0.0)
            if carry is not None:
                v = v + carry
            out.append(v)
            carry = v[7:8]
        return out

    def previous(values):
        out, carry = [], jnp.zeros((1, 128), jnp.float32)
        for v in values:
            out.append(jnp.where(sub == 0, carry, pltpu.roll(v, 1, 0)))
            carry = v[7:8]
        return out

    def gather(x, index):
        return jnp.take_along_axis(x, index, axis=0, mode="promise_in_bounds")

    def remap(u):
        row = jnp.where(u < 8, u, lev)
        t = jnp.where(u < 8, lax.rem(lev - u + 2 * PEERS, PEERS), 8)
        lax.fori_loop(
            0,
            PEERS - 1,
            lambda k, z: (
                remote(
                    fwd.at[0, 0], got.at[u, lev], fwd_send.at[u, k], fwd_recv.at[u, k], (lat, peer(k))
                ).wait_recv(),
                z,
            )[1],
            0,
        )

        def split(n):
            xs = [got[u, p, :, lane(n)] for p in range(PEERS)]
            first = [jnp.where(small, xs[2 * i], flip(xs[2 * i + 1])) for i in range(4)]
            second = [jnp.where(small, flip(xs[2 * i]), xs[2 * i + 1]) for i in range(4)]
            return first, second

        zonal, meridional = split(0)
        temp, tracer = split(1)
        layer = [jnp.exp(jnp.where(small, got[u, 2 * i, :, lane(2)], got[u, 2 * i + 1, :, lane(2)])) for i in range(4)]
        lower = running(layer)
        upper = [x - y for x, y in zip(lower, layer)]
        bottom = lower[3][7:8]
        fields = (zonal, meridional, temp, tracer)
        before = []
        for f in fields:
            weighted = [x * y for x, y in zip(f, layer)]
            before.append([x - y for x, y in zip(running(weighted), weighted)])
        target = [bottom * bound[8 * i : 8 * i + 8, :] for i in range(4)]
        integral = [[] for _ in fields]
        ends = [lower[m][7:8] for m in range(3)]
        mids = [jnp.broadcast_to(lower[m][3:4], (8, 128)) for m in range(4)]
        for i in range(4):
            goal = target[i]
            past = [goal > e for e in ends]

            def pick(q):
                return jnp.where(past[2], q[3], jnp.where(past[1], q[2], jnp.where(past[0], q[1], q[0])))

            pos = jnp.where(pick(mids) < goal, 4, 0)
            pos = pos + jnp.where(pick([gather(x, pos + 1) for x in lower]) < goal, 2, 0)
            pos = pos + jnp.where(pick([gather(x, pos) for x in lower]) < goal, 1, 0)

            def here(q):
                return pick([gather(x, pos) for x in q])

            depth = goal - here(upper)
            for n, f in enumerate(fields):
                integral[n].append(here(before[n]) + depth * here(f))
        new_thick = [bottom * share[8 * i : 8 * i + 8, :] for i in range(4)]
        inverse = [1.0 / x for x in new_thick]
        remapped = [[(x - y) * z for x, y, z in zip(g, previous(g), inverse)] for g in integral]
        rise = [
            r * jnp.log((TOP_PRESSURE + x) / (TOP_PRESSURE + y))
            for r, x, y in zip(remapped[2], target, previous(target))
        ]
        geo = [None] * 4
        ground = surf[:, pl.ds(pl.multiple_of(t * 128, 128), 128)]
        carry = jnp.sum(jnp.where(sub == row, ground, 0.0), axis=0, keepdims=True)
        for i in (3, 2, 1, 0):
            x = rise[i]
            for d in (1, 2, 4):
                x = x + jnp.where(sub < 8 - d, pltpu.roll(x, 8 - d, 0), 0.0)
            geo[i] = x + carry
            carry = geo[i][0:1]
        pairs = ((remapped[0], remapped[1]), (remapped[2], remapped[3]), (geo, new_thick))
        for n, (one, two) in enumerate(pairs):
            for i in range(4):
                ret[u, 2 * i, :, lane(n)] = jnp.where(small, one[i], flip(two[i]))
                ret[u, 2 * i + 1, :, lane(n)] = jnp.where(small, flip(one[i]), two[i])
        lax.fori_loop(0, PEERS - 1, lambda k, z: (ret_copy(u, row, t, k).start(), z)[1], 0)
        back[t, row] = ret[u, lev]

    lax.fori_loop(5, 7, lambda m, z: (substep(1, 2 * m, 2 * m + 1), z)[1], 0)

    def front(h, depth):
        receive(0, h)
        receive(1, h)
        for n in range(1, min(depth, 3) + 1):
            substep(n, 8 + 2 * n - h, 15 - 2 * n + h)
        if depth == 4:
            release(8 - h, h - 1)

    def fronts(first, depth):
        def body(m, carry):
            h = first + 2 * m
            if relayed:
                pass_on(h + 1)
            front(h, depth)
            front(h + 1, depth)
            return carry

        return body

    lax.fori_loop(0, 1, fronts(1, 2), 0)
    lax.fori_loop(0, 1, fronts(3, 3), 0)
    lax.fori_loop(0, 2, fronts(5, 4), 0)

    def unit(n, carry):
        q = n // 2
        remap(jnp.where(n == 8, 8, jnp.where(n == 2 * q, 3 - q, 4 + q)))
        return carry

    lax.fori_loop(0, 9, unit, 0)

    def arrived(n, carry):
        u, k = n // (PEERS - 1), lax.rem(n, PEERS - 1)
        ret_copy(u, 0, 0, k).wait()
        return carry

    lax.fori_loop(0, 9 * (PEERS - 1), arrived, 0)

    def deliver(t, carry):
        for n in range(3):
            xs = [back[t, r, :, lane(n)] for r in range(ROWS)]
            for i, x in enumerate(transposed(xs)):
                result[64 * n + 8 * i : 64 * n + 8 * i + 8, pl.ds(pl.multiple_of(t * 128, 128), 128)] = x
        return carry

    lax.fori_loop(0, TILES, deliver, 0)

    outs = [
        pltpu.make_async_copy(result.at[pl.ds(at, size)], ref, out_sem.at[n])
        for n, (ref, at, size) in enumerate(((out_ref, 0, 128), (out_geo_ref, 128, 32), (out_thick_ref, 160, 32)))
    ]
    for copy in outs:
        copy.start()

    def sent(n, carry):
        u, k = n // (PEERS - 1), lax.rem(n, PEERS - 1)
        remote(fwd.at[0, 0], got.at[0, lev], fwd_send.at[u, k], fwd_recv.at[u, k], (lat, peer(k))).wait_send()
        return carry

    lax.fori_loop(0, 9 * (PEERS - 1), sent, 0)
    for h in range(1, ROWS + 1):
        pl.when(has_south)(lambda h=h: to_south(h).wait_send())
        pl.when(has_north)(lambda h=h: to_north(h).wait_send())
    if relayed:
        for h in range(2, ROWS + 1, 2):
            pl.when(relays_south)(lambda h=h: forward_south(h).wait_send())
            pl.when(relays_north)(lambda h=h: forward_north(h).wait_send())
    for copy in outs:
        copy.wait()


def shards(lat_size, velocity, potential_temp, tracer, thickness, surface_height, level_fractions):
    hbm = pl.BlockSpec(memory_space=pltpu.HBM)
    f32 = jnp.float32
    remapped, new_thickness, geopotential = pl.pallas_call(
        functools.partial(kernel, lat_size),
        out_shape=(
            jax.ShapeDtypeStruct((128, LON), f32),
            jax.ShapeDtypeStruct((32, LON), f32),
            jax.ShapeDtypeStruct((32, LON), f32),
        ),
        in_specs=[hbm] * 6,
        out_specs=(hbm,) * 3,
        scratch_shapes=[
            pltpu.SMEM((32,), f32),
            pltpu.VMEM((160, LON), f32),
            pltpu.VMEM((3 * ROWS, 8, ROW), f32),
            *[pltpu.VMEM((3 * ROWS, 8, LON), f32)] * 10,
            pltpu.VMEM((3 * ROWS, 8, 128), f32),
            pltpu.VMEM((32, 128), f32),
            pltpu.VMEM((32, 128), f32),
            pltpu.VMEM((ROWS, LON), f32),
            pltpu.VMEM((ROWS // 2, 8, ROW), f32),
            pltpu.VMEM((ROWS, TILES, 8, PIECE), f32),
            pltpu.VMEM((TILES, PEERS, 8, PIECE), f32),
            pltpu.VMEM((TILES, PEERS, 8, PIECE), f32),
            pltpu.VMEM((TILES, ROWS, 8, PIECE), f32),
            pltpu.VMEM((192, LON), f32),
            pltpu.SemaphoreType.DMA((6,)),
            pltpu.SemaphoreType.DMA((2, ROWS)),
            pltpu.SemaphoreType.DMA((2, ROWS)),
            pltpu.SemaphoreType.DMA((ROWS // 2,)),
            pltpu.SemaphoreType.DMA((ROWS // 2,)),
            pltpu.SemaphoreType.DMA((9, PEERS - 1)),
            pltpu.SemaphoreType.DMA((9, PEERS - 1)),
            pltpu.SemaphoreType.DMA((9, PEERS - 1)),
            pltpu.SemaphoreType.DMA((9, PEERS - 1)),
            pltpu.SemaphoreType.DMA((3,)),
        ],
        compiler_params=pltpu.CompilerParams(
            collective_id=0, has_side_effects=True, vmem_limit_bytes=63 * 2**20
        ),
        cost_estimate=pl.CostEstimate(flops=10**8, bytes_accessed=2 * 10**6, transcendentals=10**6),
    )(
        velocity.reshape(64, LON),
        potential_temp.reshape(32, LON),
        tracer.reshape(32, LON),
        thickness.reshape(32, LON),
        surface_height,
        level_fractions,
    )
    return (
        remapped.reshape(4, 4, ROWS, LON),
        new_thickness.reshape(4, ROWS, LON),
        geopotential.reshape(4, ROWS, LON),
    )


def solution(mesh):
    return jax.shard_map(
        functools.partial(shards, mesh.shape["lat"]),
        mesh=mesh,
        in_specs=(
            P(None, "lev", "lat", None),
            P("lev", "lat", None),
            P("lev", "lat", None),
            P("lev", "lat", None),
            P("lat", None),
            P(),
        ),
        out_specs=(P(None, "lev", "lat", None), P("lev", "lat", None), P("lev", "lat", None)),
        check_vma=False,
    )
```

```python
import functools
import math

import jax
import jax.numpy as jnp
from jax import lax
from jax.experimental import pallas as pl
from jax.experimental.pallas import tpu as pltpu
from jax.sharding import PartitionSpec as P

MESH = pl.DeviceIdType.MESH
SUBSTEPS = 4
ADVECT = 0.3 / 12.0
PRESS = 0.15 / 12.0
ROTATION_RATE = 0.3
TOP_PRESSURE = 1.0

ROWS = 8
LON = 1152
TILES = 9
ROW = 2 * LON + 640
PIECE = 384
PAIR = 640
PEERS = 8
RING = 8
RELAYED = (3, 5, 7)


def kernel(
    lat_size,
    vel_ref, temp_ref, tracer_ref, thick_ref, surf_ref, frac_ref,
    out_ref, out_thick_ref, out_geo_ref,
    frac, band, rows, s_0, uv_1, pq_1, s_1, uv_2, pq_2, s_2, uv_3, pq_3, s_3, turn, bound, share, splat, surf,
    relay, fwd, extra, s_4, got, ret, bottoms, back,
    local_sem, halo_send, halo_recv, relay_send, relay_recv, fwd_send, fwd_recv, ret_send, ret_recv,
):
    lat, lev = lax.axis_index("lat"), lax.axis_index("lev")
    relayed = lat_size % RING == 0 and lat_size > RING

    def band_at(offset):
        return lax.rem(lat + offset + lat_size, lat_size)

    def lane(t):
        return slice(128 * t, 128 * t + 128)

    parts = ((vel_ref, 0, 64), (temp_ref, 64, 32), (tracer_ref, 96, 32), (thick_ref, 128, 32))
    own = [
        pltpu.make_async_copy(ref, band.at[pl.ds(at, size)], local_sem.at[n])
        for n, (ref, at, size) in enumerate(parts)
    ]
    later = [
        pltpu.make_async_copy(surf_ref, surf, local_sem.at[4]),
        pltpu.make_async_copy(frac_ref, frac, local_sem.at[5]),
    ]
    for copy in own + later:
        copy.start()

    has_north, has_south = lat > 0, lat < lat_size - 1
    before_step = lax.rem(lat, RING) == RING - 1
    after_step = lax.rem(lat, RING) == 0
    beside = band_at(jnp.where(before_step, 1 - RING, RING - 1))
    ahead, behind = lat + RING < lat_size, lat >= RING
    relays_south = after_step & ahead
    relays_north = before_step & behind

    barrier = pltpu.get_barrier_semaphore()

    def greet(row):
        pl.semaphore_signal(barrier, inc=1, device_id=(row, lev), device_id_type=MESH)

    def peer(step):
        return lax.rem(lev + 1 + step, PEERS)

    pl.when(has_north)(lambda: greet(band_at(-1)))
    pl.when(has_south)(lambda: greet(band_at(1)))
    for step in range(PEERS - 1):
        pl.semaphore_signal(barrier, inc=1, device_id=(lat, peer(step)), device_id_type=MESH)
    guests = PEERS - 1 + jnp.where(has_north, 1, 0) + jnp.where(has_south, 1, 0)
    if relayed:

        @pl.when(before_step | after_step)
        def _():
            greet(beside)
            pl.when(ahead)(lambda: greet(band_at(RING)))
            pl.when(behind)(lambda: greet(band_at(-RING)))

        more = 1 + jnp.where(ahead, 1, 0) + jnp.where(behind, 1, 0)
        guests = guests + jnp.where(before_step | after_step, more, 0)

    sub = lax.broadcasted_iota(jnp.int32, (8, 128), 0)
    lanes_in = lax.broadcasted_iota(jnp.int32, (8, 128), 1)
    small = sub < 4

    def flip(x):
        return pltpu.roll(x, 4, 0)

    def transposed(xs):
        for d in (4, 2, 1):
            ys = list(xs)
            for i in range(8):
                if not i & d:
                    ys[i] = jnp.where(sub & d == 0, xs[i], pltpu.roll(xs[i + d], d, 0))
                    ys[i + d] = jnp.where(sub & d == 0, pltpu.roll(xs[i], 8 - d, 0), xs[i + d])
            xs = ys
        return xs

    for copy in own:
        copy.wait()

    def unpack(t, carry):
        at = pl.multiple_of(t * 128, 128)
        for start, n in ((0, 0), (LON, 64)):
            xs = [band[n + 8 * i : n + 8 * i + 8, pl.ds(at, 128)] for i in range(8)]
            for r, x in enumerate(transposed(xs)):
                rows[ROWS + r, :, pl.ds(start + at, 128)] = x
        xs = [jnp.log(band[128 + 8 * i : 136 + 8 * i, pl.ds(at, 128)]) for i in range(4)]
        for r, x in enumerate(transposed(xs + xs)):
            s_0[ROWS + r, :, pl.ds(at, 128)] = x
        return carry

    lax.fori_loop(0, TILES, unpack, 0)

    def fold(r, carry):
        j = ROWS + r
        for t in range(4):
            x = jnp.where(small, s_0[j, :, lane(t)], s_0[j, :, lane(t + 5)])
            rows[j, :, 2 * LON + 128 * t : 2 * LON + 128 * (t + 1)] = x
        rows[j, :, 2 * LON + 512 :] = s_0[j, :, lane(4)]
        return carry

    lax.fori_loop(0, ROWS, fold, 0)

    pl.semaphore_wait(barrier, guests)

    def remote(src, dst, send, recv, to):
        return pltpu.make_async_remote_copy(
            src_ref=src, dst_ref=dst, send_sem=send, recv_sem=recv, device_id=to, device_id_type=MESH
        )

    def to_south(h, src=None, row=None, send=None):
        return remote(
            rows.at[2 * ROWS - h] if src is None else src,
            rows.at[ROWS - h],
            halo_send.at[0, h - 1] if send is None else send,
            halo_recv.at[0, h - 1],
            (band_at(1) if row is None else row, lev),
        )

    def to_north(h, src=None, row=None, send=None):
        return remote(
            rows.at[ROWS - 1 + h] if src is None else src,
            rows.at[2 * ROWS - 1 + h],
            halo_send.at[1, h - 1] if send is None else send,
            halo_recv.at[1, h - 1],
            (band_at(-1) if row is None else row, lev),
        )

    def to_relay(way, h):
        n = RELAYED.index(h)
        src = rows.at[2 * ROWS - h] if way == 0 else rows.at[ROWS - 1 + h]
        return remote(src, relay.at[n], halo_send.at[way, h - 1], relay_recv.at[n], (beside, lev))

    for h in range(1, ROWS + 1):
        if relayed and h in RELAYED:
            pl.when(has_south & before_step)(lambda h=h: to_relay(0, h).start())
            pl.when(has_south & jnp.logical_not(before_step))(lambda h=h: to_south(h).start())
            pl.when(has_north & after_step)(lambda h=h: to_relay(1, h).start())
            pl.when(has_north & jnp.logical_not(after_step))(lambda h=h: to_north(h).start())
        else:
            pl.when(has_south)(lambda h=h: to_south(h).start())
            pl.when(has_north)(lambda h=h: to_north(h).start())

    def forward_south(h):
        return to_south(h, relay.at[RELAYED.index(h)], band_at(RING), relay_send.at[RELAYED.index(h)])

    def forward_north(h):
        return to_north(h, relay.at[RELAYED.index(h)], band_at(-RING), relay_send.at[RELAYED.index(h)])

    def pass_on(h):
        @pl.when(relays_south)
        def _():
            to_relay(0, h).wait_recv()
            forward_south(h).start()

        @pl.when(relays_north)
        def _():
            to_relay(1, h).wait_recv()
            forward_north(h).start()

    for copy in later:
        copy.wait()
    total = jnp.float32(0.0)
    for k in range(4 * PEERS):
        total = total + frac[k]
        share[k, :] = jnp.full((128,), frac[k], jnp.float32)
        splat[k] = jnp.full((8, 128), frac[k], jnp.float32)
        bound[k, :] = jnp.full((128,), total, jnp.float32)
    share[...] = share[...] / total
    bound[...] = bound[...] / total
    bottoms[...] = jnp.zeros((8, 128), jnp.float32)
    row_of = lax.broadcasted_iota(jnp.int32, (3 * ROWS, 8, 128), 0) + (lat - 1) * ROWS
    angle = -0.5 * math.pi + (row_of.astype(jnp.float32) + 0.5) * (math.pi / (lat_size * ROWS))
    sign = jnp.where(lax.broadcasted_iota(jnp.int32, (3 * ROWS, 8, 128), 1) < 4, ROTATION_RATE, -ROTATION_RATE)
    turn[...] = sign * jnp.sin(angle)

    def inside(j):
        row = (lat - 1) * ROWS + j
        return jnp.where((row >= 0) & (row < lat_size * ROWS), 1.0, 0.0).astype(jnp.float32)

    def advance(state, js, emits):
        (uv_ref, _), (pq_ref, pq_at), (s_ref, _) = state
        fields = ((uv_ref, 0), (pq_ref, pq_at), (s_ref, 0))

        def line(j, emit):
            spin = turn[j]

            def load(n, row, t):
                ref, at = fields[n]
                return ref[row, :, at + 128 * t : at + 128 * (t + 1)]

            here, rolled = {}, {}

            def value(n, t):
                if (n, t) not in here:
                    here[n, t] = load(n, j, t)
                return here[n, t]

            def roll(n, t, k):
                t = t % TILES
                if (n, t, k) not in rolled:
                    rolled[n, t, k] = pltpu.roll(value(n, t), k, 1)
                return rolled[n, t, k]

            def east(n, t):
                one = jnp.where(lanes_in < 127, roll(n, t, 127), roll(n, t + 1, 127)) - jnp.where(
                    lanes_in < 1, roll(n, t - 1, 1), roll(n, t, 1)
                )
                two = jnp.where(lanes_in < 126, roll(n, t, 126), roll(n, t + 1, 126)) - jnp.where(
                    lanes_in < 2, roll(n, t - 1, 2), roll(n, t, 2)
                )
                return 8.0 * one - two

            def up(n, t):
                return 8.0 * (load(n, j + 1, t) - load(n, j - 1, t)) - (load(n, j + 2, t) - load(n, j - 2, t))

            def step(t):
                uv, pq, s = (value(n, t) for n in range(3))
                turned = flip(uv)
                eastward = jnp.where(small, uv, turned) * ADVECT
                northward = jnp.where(small, turned, uv) * ADVECT
                uv_east, uv_up = east(0, t), up(0, t)
                s_east, s_up = east(2, t), up(2, t)
                new_pq = pq - eastward * east(1, t) - northward * up(1, t)
                push = PRESS * jnp.where(small, s_east, s_up)
                new_uv = uv - eastward * uv_east - northward * uv_up - push + spin * turned
                spread = jnp.where(small, uv_east, uv_up)
                new_s = s - eastward * s_east - northward * s_up - ADVECT * (spread + flip(spread))
                emit(t, new_uv, new_pq, new_s)

            return step

        steps = [line(j, emit) for j, emit in zip(js, emits)]
        for t in range(TILES):
            for step in steps:
                step(t)

    states = (
        ((rows, 0), (rows, LON), (s_0, 0)),
        ((uv_1, 0), (pq_1, 0), (s_1, 0)),
        ((uv_2, 0), (pq_2, 0), (s_2, 0)),
        ((uv_3, 0), (pq_3, 0), (s_3, 0)),
    )

    def substep(n, *js):
        dst = states[n]

        def into(j):
            keep = inside(j)

            def emit(t, new_uv, new_pq, new_s):
                dst[0][0][j, :, lane(t)] = new_uv * keep
                dst[1][0][j, :, lane(t)] = new_pq
                dst[2][0][j, :, lane(t)] = new_s * keep

            return emit

        advance(states[n - 1], js, [into(j) for j in js])

    def receive(way, h):
        j = ROWS - h if way == 0 else 2 * ROWS - 1 + h
        there = has_north if way == 0 else has_south
        pl.when(there)(lambda: (to_south(h) if way == 0 else to_north(h)).wait_recv())

        @pl.when(jnp.logical_not(there))
        def _():
            rows[j] = jnp.zeros((8, ROW), jnp.float32)

        for t in range(5):
            x = rows[j, :, 2 * LON + 128 * t : 2 * LON + 128 * (t + 1)]
            y = flip(x)
            s_0[j, :, lane(t)] = jnp.where(small, x, y)
            if t < 4:
                s_0[j, :, lane(t + 5)] = jnp.where(small, y, x)

    def fwd_copy(q, step):
        to = peer(step)
        return remote(fwd.at[q, to], got.at[q, lev], fwd_send.at[q, step], fwd_recv.at[q, step], (lat, to))

    def extra_copy(q, side, to, step):
        dst = got.at[4, lev, :, pl.ds(0, PIECE)]
        return remote(extra.at[q, side], dst, fwd_send.at[4, step], fwd_recv.at[4, step], (lat, to))

    def release(q):
        pair = (3 - q, 4 + q)

        def into(side, r):
            at = side * PIECE

            def emit(t, new_uv, new_pq, new_s):
                if t < 8:
                    to = lax.rem(r + t, PEERS)
                    fwd[q, to, :, at : at + 128] = new_uv
                    fwd[q, to, :, at + 128 : at + 256] = new_pq
                    s_4[side, to] = new_s
                else:
                    extra[q, side, :, lane(0)] = new_uv
                    extra[q, side, :, lane(1)] = new_pq
                    extra[q, side, :, lane(2)] = new_s

            return emit

        advance(states[3], [ROWS + r for r in pair], [into(side, r) for side, r in enumerate(pair)])
        for to in range(PEERS):
            fwd[q, to, :, lane(2)] = jnp.where(small, s_4[0, to], s_4[1, to])
        lax.fori_loop(0, PEERS - 1, lambda k, z: (fwd_copy(q, k).start(), z)[1], 0)
        got[q, lev] = fwd[q, lev]
        for side, r in enumerate(pair):
            step = lax.rem(r - lev - 1 + 2 * PEERS, PEERS)
            pl.when(r != lev)(lambda side=side, r=r, step=step: extra_copy(q, side, r, step).start())

            @pl.when(r == lev)
            def _(side=side):
                got[4, lev, :, 0:PIECE] = extra[q, side]

    def ret_copy(q, step):
        to = peer(step)
        return remote(ret.at[q, to], back.at[q, lev], ret_send.at[q, step], ret_recv.at[q, step], (lat, to))

    def last_copy(step):
        to, lanes = peer(step), pl.ds(0, 512)
        dst = back.at[4, lev, :, lanes]
        return remote(ret.at[4, to, :, lanes], dst, ret_send.at[4, step], ret_recv.at[4, step], (lat, to))

    def running(values):
        out, carry = [], None
        for v in values:
            for d in (1, 2, 4):
                v = v + jnp.where(sub >= d, pltpu.roll(v, d, 0), 0.0)
            if carry is not None:
                v = v + carry
            out.append(v)
            carry = v[7:8]
        return out

    def previous(values):
        out, carry = [], jnp.zeros((1, 128), jnp.float32)
        for v in values:
            out.append(jnp.where(sub == 0, carry, pltpu.roll(v, 1, 0)))
            carry = v[7:8]
        return out

    def gather(x, index):
        return jnp.take_along_axis(x, index, axis=0, mode="promise_in_bounds")

    def remap(q, side):
        first = side == 0
        row = jnp.where(q == 4, lev, jnp.where(first, 3 - q, 4 + q))
        t = jnp.where(q == 4, 8, lax.rem(lev - row + 2 * PEERS, PEERS))
        at = side * PIECE

        def split(n):
            xs = [got[q, p, :, pl.ds(pl.multiple_of(at + 128 * n, 128), 128)] for p in range(PEERS)]
            one = [jnp.where(small, xs[2 * i], flip(xs[2 * i + 1])) for i in range(4)]
            two = [jnp.where(small, flip(xs[2 * i]), xs[2 * i + 1]) for i in range(4)]
            return one, two

        zonal, meridional = split(0)
        temp, tracer = split(1)
        xs = [got[q, p, :, lane(2)] for p in range(PEERS)]
        layer = []
        for i in range(4):
            one = jnp.where(small, xs[2 * i], flip(xs[2 * i + 1]))
            two = jnp.where(small, flip(xs[2 * i]), xs[2 * i + 1])
            layer.append(jnp.exp(jnp.where(first, one, two)))
        lower = running(layer)
        upper = [x - y for x, y in zip(lower, layer)]
        bottom = lower[3][7:8]
        fields = (zonal, meridional, temp, tracer)
        before = []
        for f in fields:
            weighted = [x * y for x, y in zip(f, layer)]
            before.append([x - y for x, y in zip(running(weighted), weighted)])
        target = [bottom * bound[8 * i : 8 * i + 8, :] for i in range(4)]
        integral = [[] for _ in fields]
        ends = [lower[m][7:8] for m in range(3)]
        mids = [jnp.broadcast_to(lower[m][3:4], (8, 128)) for m in range(4)]
        for i in range(4):
            goal = target[i]
            past = [goal > e for e in ends]

            def pick(x):
                return jnp.where(past[2], x[3], jnp.where(past[1], x[2], jnp.where(past[0], x[1], x[0])))

            pos = jnp.where(pick(mids) < goal, 4, 0)
            pos = pos + jnp.where(pick([gather(x, pos + 1) for x in lower]) < goal, 2, 0)
            pos = pos + jnp.where(pick([gather(x, pos) for x in lower]) < goal, 1, 0)

            def here(xs):
                return pick([gather(x, pos) for x in xs])

            depth = goal - here(upper)
            for n, f in enumerate(fields):
                integral[n].append(here(before[n]) + depth * here(f))
        new_thick = [bottom * share[8 * i : 8 * i + 8, :] for i in range(4)]
        inverse = [1.0 / x for x in new_thick]
        remapped = [[(x - y) * z for x, y, z in zip(g, previous(g), inverse)] for g in integral]
        rise = [
            r * jnp.log((TOP_PRESSURE + x) / (TOP_PRESSURE + y))
            for r, x, y in zip(remapped[2], target, previous(target))
        ]
        geo = [None] * 4
        ground = surf[:, pl.ds(pl.multiple_of(t * 128, 128), 128)]
        carry = jnp.sum(jnp.where(sub == row, ground, 0.0), axis=0, keepdims=True)
        for i in (3, 2, 1, 0):
            x = rise[i]
            for d in (1, 2, 4):
                x = x + jnp.where(sub < 8 - d, pltpu.roll(x, 8 - d, 0), 0.0)
            geo[i] = x + carry
            carry = geo[i][0:1]
        for n, (one, two) in enumerate(((remapped[0], remapped[1]), (remapped[2], remapped[3]))):
            lanes = pl.ds(pl.multiple_of(at + 128 * n, 128), 128)
            for i in range(4):
                ret[q, 2 * i, :, lanes] = jnp.where(small, one[i], flip(two[i]))
                ret[q, 2 * i + 1, :, lanes] = jnp.where(small, flip(one[i]), two[i])
        mine = jnp.where(first, sub, 7 - sub) < 4
        floor = jnp.broadcast_to(bottom, (8, 128))
        for i in range(4):
            flipped = flip(geo[i])
            for p, x in ((2 * i, jnp.where(first, geo[i], flipped)), (2 * i + 1, jnp.where(first, flipped, geo[i]))):
                other = jnp.where(first, floor, ret[q, p, :, lane(2)])
                ret[q, p, :, lane(2)] = jnp.where(mine, x, other)
        bottoms[...] = jnp.where((sub == row) & (q < 4), floor, bottoms[...])

    def process(q):
        lax.fori_loop(0, PEERS - 1, lambda k, z: (fwd_copy(q, k).wait_recv(), z)[1], 0)
        lax.fori_loop(0, 2, lambda side, z: (remap(q, side), z)[1], 0)
        lax.fori_loop(0, PEERS - 1, lambda k, z: (ret_copy(q, k).start(), z)[1], 0)
        back[q, lev] = ret[q, lev]

    lax.fori_loop(5, 7, lambda m, z: (substep(1, 2 * m, 2 * m + 1), z)[1], 0)

    def front(h, depth):
        receive(0, h)
        receive(1, h)
        for n in range(1, min(depth, 3) + 1):
            substep(n, 8 + 2 * n - h, 15 - 2 * n + h)
        if depth == 4:
            release(h - 5)

    def passing(h):
        if relayed:
            pass_on(h)

    def late(m, carry):
        front(5 + 2 * m, 4)
        pl.when(m == 1)(lambda: process(0))
        front(6 + 2 * m, 4)
        pl.when(m == 1)(lambda: process(1))
        return carry

    passing(3)
    front(1, 2)
    passing(5)
    front(2, 2)
    passing(7)
    front(3, 3)
    front(4, 3)
    lax.fori_loop(0, 2, late, 0)
    lax.fori_loop(2, 4, lambda q, z: (process(q), z)[1], 0)
    lax.fori_loop(0, PEERS - 1, lambda k, z: (extra_copy(0, 0, 0, k).wait_recv(), z)[1], 0)
    remap(4, 0)
    for p in range(PEERS):
        ret[4, p, :, lane(3)] = bottoms[...]
    lax.fori_loop(0, PEERS - 1, lambda k, z: (last_copy(k).start(), z)[1], 0)
    back[4, lev, :, 0:512] = ret[4, lev, :, 0:512]

    for q in range(4):
        lax.fori_loop(0, PEERS - 1, lambda k, z, q=q: (ret_copy(q, k).wait(), z)[1], 0)
    lax.fori_loop(0, PEERS - 1, lambda k, z: (last_copy(k).wait(), z)[1], 0)

    def put(lanes, uv, pq, geo, bottom):
        for at, xs in ((0, uv), (64, pq)):
            for i, x in enumerate(transposed(xs)):
                out_ref[at + 8 * i : at + 8 * i + 8, lanes] = x
        for i, x in enumerate(transposed(geo)[:4]):
            out_geo_ref[8 * i : 8 * i + 8, lanes] = x
            out_thick_ref[8 * i : 8 * i + 8, lanes] = bottom * (splat[4 * lev + i] / total)

    def deliver(t, carry):
        uv, pq, geo = [], [], []
        bottom = jnp.zeros((8, 128), jnp.float32)
        for r in range(ROWS):
            owner, q, side = lax.rem(r + t, PEERS), max(3 - r, r - 4), r // 4
            uv.append(back[q, owner, :, side * PIECE : side * PIECE + 128])
            pq.append(back[q, owner, :, side * PIECE + 128 : side * PIECE + 256])
            x = back[q, owner, :, lane(2)]
            geo.append(flip(x) if side else x)
            bottom = jnp.where(sub == r, back[4, owner, :, lane(3)], bottom)
        put(pl.ds(pl.multiple_of(t * 128, 128), 128), uv, pq, geo, bottom)
        return carry

    lax.fori_loop(0, TILES - 1, deliver, 0)
    geo = [back[4, r, :, lane(2)] for r in range(ROWS)]
    bottom = jnp.zeros((8, 128), jnp.float32)
    for r in range(ROWS):
        bottom = jnp.where(sub == r, geo[r] if r >= 4 else flip(geo[r]), bottom)
    put(
        lane(8),
        [back[4, r, :, lane(0)] for r in range(ROWS)],
        [back[4, r, :, lane(1)] for r in range(ROWS)],
        geo,
        bottom,
    )

    for q in range(4):
        lax.fori_loop(0, PEERS - 1, lambda k, z, q=q: (fwd_copy(q, k).wait_send(), z)[1], 0)
    lax.fori_loop(0, PEERS - 1, lambda k, z: (extra_copy(0, 0, 0, k).wait_send(), z)[1], 0)
    for h in range(1, ROWS + 1):
        pl.when(has_south)(lambda h=h: to_south(h).wait_send())
        pl.when(has_north)(lambda h=h: to_north(h).wait_send())
    if relayed:
        for h in RELAYED:
            pl.when(relays_south)(lambda h=h: forward_south(h).wait_send())
            pl.when(relays_north)(lambda h=h: forward_north(h).wait_send())


def shards(lat_size, velocity, potential_temp, tracer, thickness, surface_height, level_fractions):
    hbm = pl.BlockSpec(memory_space=pltpu.HBM)
    f32 = jnp.float32
    remapped, new_thickness, geopotential = pl.pallas_call(
        functools.partial(kernel, lat_size),
        out_shape=(
            jax.ShapeDtypeStruct((128, LON), f32),
            jax.ShapeDtypeStruct((32, LON), f32),
            jax.ShapeDtypeStruct((32, LON), f32),
        ),
        in_specs=[hbm] * 6,
        out_specs=(pl.BlockSpec(memory_space=pltpu.VMEM),) * 3,
        scratch_shapes=[
            pltpu.SMEM((32,), f32),
            pltpu.VMEM((160, LON), f32),
            pltpu.VMEM((3 * ROWS, 8, ROW), f32),
            *[pltpu.VMEM((3 * ROWS, 8, LON), f32)] * 10,
            pltpu.VMEM((3 * ROWS, 8, 128), f32),
            pltpu.VMEM((32, 128), f32),
            pltpu.VMEM((32, 128), f32),
            pltpu.VMEM((32, 8, 128), f32),
            pltpu.VMEM((ROWS, LON), f32),
            pltpu.VMEM((len(RELAYED), 8, ROW), f32),
            pltpu.VMEM((4, PEERS, 8, PAIR), f32),
            pltpu.VMEM((4, 2, 8, PIECE), f32),
            pltpu.VMEM((2, PEERS, 8, 128), f32),
            pltpu.VMEM((5, PEERS, 8, PAIR), f32),
            pltpu.VMEM((5, PEERS, 8, PAIR), f32),
            pltpu.VMEM((8, 128), f32),
            pltpu.VMEM((5, PEERS, 8, PAIR), f32),
            pltpu.SemaphoreType.DMA((6,)),
            pltpu.SemaphoreType.DMA((2, ROWS)),
            pltpu.SemaphoreType.DMA((2, ROWS)),
            pltpu.SemaphoreType.DMA((len(RELAYED),)),
            pltpu.SemaphoreType.DMA((len(RELAYED),)),
            pltpu.SemaphoreType.DMA((5, PEERS - 1)),
            pltpu.SemaphoreType.DMA((5, PEERS - 1)),
            pltpu.SemaphoreType.DMA((5, PEERS - 1)),
            pltpu.SemaphoreType.DMA((5, PEERS - 1)),
        ],
        compiler_params=pltpu.CompilerParams(
            collective_id=0, has_side_effects=True, vmem_limit_bytes=64 * 2**20 - 6 * 32 * LON * 4 - 4096
        ),
        cost_estimate=pl.CostEstimate(flops=10**8, bytes_accessed=2 * 10**6, transcendentals=10**6),
    )(
        velocity.reshape(64, LON),
        potential_temp.reshape(32, LON),
        tracer.reshape(32, LON),
        thickness.reshape(32, LON),
        surface_height,
        level_fractions,
    )
    return (
        remapped.reshape(4, 4, ROWS, LON),
        new_thickness.reshape(4, ROWS, LON),
        geopotential.reshape(4, ROWS, LON),
    )


def solution(mesh):
    return jax.shard_map(
        functools.partial(shards, mesh.shape["lat"]),
        mesh=mesh,
        in_specs=(
            P(None, "lev", "lat", None),
            P("lev", "lat", None),
            P("lev", "lat", None),
            P("lev", "lat", None),
            P("lat", None),
            P(),
        ),
        out_specs=(P(None, "lev", "lat", None), P("lev", "lat", None), P("lev", "lat", None)),
        check_vma=False,
    )
```

```python
import functools
import math

import jax
import jax.numpy as jnp
from jax import lax
from jax.experimental import pallas as pl
from jax.experimental.pallas import tpu as pltpu
from jax.sharding import PartitionSpec as P

MESH = pl.DeviceIdType.MESH
SUBSTEPS = 4
ADVECT = 0.3 / 12.0
PRESS = 0.15 / 12.0
ROTATION_RATE = 0.3
TOP_PRESSURE = 1.0

ROWS = 8
LON = 1152
TILES = 9
ROW = 2 * LON + 640
PIECE = 384
PAIR = 640
PEERS = 8
RING = 8
RELAYED = (3, 5, 7)


def kernel(
    lat_size,
    vel_ref, temp_ref, tracer_ref, thick_ref, surf_ref, frac_ref,
    out_ref, out_thick_ref, out_geo_ref,
    frac, band, rows, s_0, uv_1, pq_1, s_1, uv_2, pq_2, s_2, uv_3, pq_3, s_3, turn, bound, share, splat, surf,
    relay, fwd, extra, s_4, got, ret, bottoms, back,
    local_sem, halo_send, halo_recv, relay_send, relay_recv, fwd_send, fwd_recv, ret_send, ret_recv,
):
    lat, lev = lax.axis_index("lat"), lax.axis_index("lev")
    relayed = lat_size % RING == 0 and lat_size > RING

    def band_at(offset):
        return lax.rem(lat + offset + lat_size, lat_size)

    def lane(t):
        return slice(128 * t, 128 * t + 128)

    parts = ((vel_ref, 0, 64), (temp_ref, 64, 32), (tracer_ref, 96, 32), (thick_ref, 128, 32))
    own = [
        pltpu.make_async_copy(ref, band.at[pl.ds(at, size)], local_sem.at[n])
        for n, (ref, at, size) in enumerate(parts)
    ]
    later = [
        pltpu.make_async_copy(surf_ref, surf, local_sem.at[4]),
        pltpu.make_async_copy(frac_ref, frac, local_sem.at[5]),
    ]
    for copy in own + later:
        copy.start()

    has_north, has_south = lat > 0, lat < lat_size - 1
    before_step = lax.rem(lat, RING) == RING - 1
    after_step = lax.rem(lat, RING) == 0
    beside = band_at(jnp.where(before_step, 1 - RING, RING - 1))
    ahead, behind = lat + RING < lat_size, lat >= RING
    relays_south = after_step & ahead
    relays_north = before_step & behind

    barrier = pltpu.get_barrier_semaphore()

    def greet(row):
        pl.semaphore_signal(barrier, inc=1, device_id=(row, lev), device_id_type=MESH)

    def peer(step):
        return lax.rem(lev + 1 + step, PEERS)

    pl.when(has_north)(lambda: greet(band_at(-1)))
    pl.when(has_south)(lambda: greet(band_at(1)))
    for step in range(PEERS - 1):
        pl.semaphore_signal(barrier, inc=1, device_id=(lat, peer(step)), device_id_type=MESH)
    guests = PEERS - 1 + jnp.where(has_north, 1, 0) + jnp.where(has_south, 1, 0)
    if relayed:

        @pl.when(before_step | after_step)
        def _():
            greet(beside)
            pl.when(ahead)(lambda: greet(band_at(RING)))
            pl.when(behind)(lambda: greet(band_at(-RING)))

        more = 1 + jnp.where(ahead, 1, 0) + jnp.where(behind, 1, 0)
        guests = guests + jnp.where(before_step | after_step, more, 0)

    sub = lax.broadcasted_iota(jnp.int32, (8, 128), 0)
    lanes_in = lax.broadcasted_iota(jnp.int32, (8, 128), 1)
    small = sub < 4

    def flip(x):
        return pltpu.roll(x, 4, 0)

    def transposed(xs):
        for d in (4, 2, 1):
            ys = list(xs)
            for i in range(8):
                if not i & d:
                    ys[i] = jnp.where(sub & d == 0, xs[i], pltpu.roll(xs[i + d], d, 0))
                    ys[i + d] = jnp.where(sub & d == 0, pltpu.roll(xs[i], 8 - d, 0), xs[i + d])
            xs = ys
        return xs

    for copy in own:
        copy.wait()

    def unpack(t, carry):
        at = pl.multiple_of(t * 128, 128)
        for start, n in ((0, 0), (LON, 64)):
            xs = [band[n + 8 * i : n + 8 * i + 8, pl.ds(at, 128)] for i in range(8)]
            for r, x in enumerate(transposed(xs)):
                rows[ROWS + r, :, pl.ds(start + at, 128)] = x
        xs = [jnp.log(band[128 + 8 * i : 136 + 8 * i, pl.ds(at, 128)]) for i in range(4)]
        for r, x in enumerate(transposed(xs + xs)):
            s_0[ROWS + r, :, pl.ds(at, 128)] = x
        return carry

    lax.fori_loop(0, TILES, unpack, 0)

    def fold(r, carry):
        j = ROWS + r
        for t in range(4):
            x = jnp.where(small, s_0[j, :, lane(t)], s_0[j, :, lane(t + 5)])
            rows[j, :, 2 * LON + 128 * t : 2 * LON + 128 * (t + 1)] = x
        rows[j, :, 2 * LON + 512 :] = s_0[j, :, lane(4)]
        return carry

    lax.fori_loop(0, ROWS, fold, 0)

    pl.semaphore_wait(barrier, guests)

    def remote(src, dst, send, recv, to):
        return pltpu.make_async_remote_copy(
            src_ref=src, dst_ref=dst, send_sem=send, recv_sem=recv, device_id=to, device_id_type=MESH
        )

    def to_south(h, src=None, row=None, send=None):
        return remote(
            rows.at[2 * ROWS - h] if src is None else src,
            rows.at[ROWS - h],
            halo_send.at[0, h - 1] if send is None else send,
            halo_recv.at[0, h - 1],
            (band_at(1) if row is None else row, lev),
        )

    def to_north(h, src=None, row=None, send=None):
        return remote(
            rows.at[ROWS - 1 + h] if src is None else src,
            rows.at[2 * ROWS - 1 + h],
            halo_send.at[1, h - 1] if send is None else send,
            halo_recv.at[1, h - 1],
            (band_at(-1) if row is None else row, lev),
        )

    def to_relay(way, h):
        n = RELAYED.index(h)
        src = rows.at[2 * ROWS - h] if way == 0 else rows.at[ROWS - 1 + h]
        return remote(src, relay.at[n], halo_send.at[way, h - 1], relay_recv.at[n], (beside, lev))

    for h in range(1, ROWS + 1):
        if relayed and h in RELAYED:
            pl.when(has_south & before_step)(lambda h=h: to_relay(0, h).start())
            pl.when(has_south & jnp.logical_not(before_step))(lambda h=h: to_south(h).start())
            pl.when(has_north & after_step)(lambda h=h: to_relay(1, h).start())
            pl.when(has_north & jnp.logical_not(after_step))(lambda h=h: to_north(h).start())
        else:
            pl.when(has_south)(lambda h=h: to_south(h).start())
            pl.when(has_north)(lambda h=h: to_north(h).start())

    def forward_south(h):
        return to_south(h, relay.at[RELAYED.index(h)], band_at(RING), relay_send.at[RELAYED.index(h)])

    def forward_north(h):
        return to_north(h, relay.at[RELAYED.index(h)], band_at(-RING), relay_send.at[RELAYED.index(h)])

    def pass_on(h):
        @pl.when(relays_south)
        def _():
            to_relay(0, h).wait_recv()
            forward_south(h).start()

        @pl.when(relays_north)
        def _():
            to_relay(1, h).wait_recv()
            forward_north(h).start()

    for copy in later:
        copy.wait()
    total = jnp.float32(0.0)
    for k in range(4 * PEERS):
        total = total + frac[k]
        share[k, :] = jnp.full((128,), frac[k], jnp.float32)
        splat[k] = jnp.full((8, 128), frac[k], jnp.float32)
        bound[k, :] = jnp.full((128,), total, jnp.float32)
    share[...] = share[...] / total
    bound[...] = bound[...] / total
    bottoms[...] = jnp.zeros((8, 128), jnp.float32)
    row_of = lax.broadcasted_iota(jnp.int32, (3 * ROWS, 8, 128), 0) + (lat - 1) * ROWS
    angle = -0.5 * math.pi + (row_of.astype(jnp.float32) + 0.5) * (math.pi / (lat_size * ROWS))
    sign = jnp.where(lax.broadcasted_iota(jnp.int32, (3 * ROWS, 8, 128), 1) < 4, ROTATION_RATE, -ROTATION_RATE)
    turn[...] = sign * jnp.sin(angle)

    def inside(j):
        row = (lat - 1) * ROWS + j
        return jnp.where((row >= 0) & (row < lat_size * ROWS), 1.0, 0.0).astype(jnp.float32)

    def advance(state, js, emits):
        (uv_ref, _), (pq_ref, pq_at), (s_ref, _) = state
        fields = ((uv_ref, 0), (pq_ref, pq_at), (s_ref, 0))

        def line(j, emit):
            spin = turn[j]

            def load(n, row, t):
                ref, at = fields[n]
                return ref[row, :, at + 128 * t : at + 128 * (t + 1)]

            here, rolled = {}, {}

            def value(n, t):
                if (n, t) not in here:
                    here[n, t] = load(n, j, t)
                return here[n, t]

            def roll(n, t, k):
                t = t % TILES
                if (n, t, k) not in rolled:
                    rolled[n, t, k] = pltpu.roll(value(n, t), k, 1)
                return rolled[n, t, k]

            def east(n, t):
                one = jnp.where(lanes_in < 127, roll(n, t, 127), roll(n, t + 1, 127)) - jnp.where(
                    lanes_in < 1, roll(n, t - 1, 1), roll(n, t, 1)
                )
                two = jnp.where(lanes_in < 126, roll(n, t, 126), roll(n, t + 1, 126)) - jnp.where(
                    lanes_in < 2, roll(n, t - 1, 2), roll(n, t, 2)
                )
                return 8.0 * one - two

            def up(n, t):
                return 8.0 * (load(n, j + 1, t) - load(n, j - 1, t)) - (load(n, j + 2, t) - load(n, j - 2, t))

            def step(t):
                uv, pq, s = (value(n, t) for n in range(3))
                turned = flip(uv)
                eastward = jnp.where(small, uv, turned) * ADVECT
                northward = jnp.where(small, turned, uv) * ADVECT
                uv_east, uv_up = east(0, t), up(0, t)
                s_east, s_up = east(2, t), up(2, t)
                new_pq = pq - eastward * east(1, t) - northward * up(1, t)
                push = PRESS * jnp.where(small, s_east, s_up)
                new_uv = uv - eastward * uv_east - northward * uv_up - push + spin * turned
                spread = jnp.where(small, uv_east, uv_up)
                new_s = s - eastward * s_east - northward * s_up - ADVECT * (spread + flip(spread))
                emit(t, new_uv, new_pq, new_s)

            return step

        steps = [line(j, emit) for j, emit in zip(js, emits)]
        for t in range(TILES):
            for step in steps:
                step(t)

    states = (
        ((rows, 0), (rows, LON), (s_0, 0)),
        ((uv_1, 0), (pq_1, 0), (s_1, 0)),
        ((uv_2, 0), (pq_2, 0), (s_2, 0)),
        ((uv_3, 0), (pq_3, 0), (s_3, 0)),
    )

    def substep(n, *js):
        dst = states[n]

        def into(j):
            keep = inside(j)

            def emit(t, new_uv, new_pq, new_s):
                dst[0][0][j, :, lane(t)] = new_uv * keep
                dst[1][0][j, :, lane(t)] = new_pq
                dst[2][0][j, :, lane(t)] = new_s * keep

            return emit

        advance(states[n - 1], js, [into(j) for j in js])

    def receive(way, h):
        j = ROWS - h if way == 0 else 2 * ROWS - 1 + h
        there = has_north if way == 0 else has_south
        pl.when(there)(lambda: (to_south(h) if way == 0 else to_north(h)).wait_recv())

        @pl.when(jnp.logical_not(there))
        def _():
            rows[j] = jnp.zeros((8, ROW), jnp.float32)

        for t in range(5):
            x = rows[j, :, 2 * LON + 128 * t : 2 * LON + 128 * (t + 1)]
            y = flip(x)
            s_0[j, :, lane(t)] = jnp.where(small, x, y)
            if t < 4:
                s_0[j, :, lane(t + 5)] = jnp.where(small, y, x)

    def fwd_copy(q, step):
        to = peer(step)
        return remote(fwd.at[q, to], got.at[q, lev], fwd_send.at[q, step], fwd_recv.at[q, step], (lat, to))

    def extra_copy(q, side, to, step):
        dst = got.at[4, lev, :, pl.ds(0, PIECE)]
        return remote(extra.at[q, side], dst, fwd_send.at[4, step], fwd_recv.at[4, step], (lat, to))

    def release(q):
        pair = (3 - q, 4 + q)

        def into(side, r):
            at = side * PIECE

            def emit(t, new_uv, new_pq, new_s):
                if t < 8:
                    to = lax.rem(r + t, PEERS)
                    fwd[q, to, :, at : at + 128] = new_uv
                    fwd[q, to, :, at + 128 : at + 256] = new_pq
                    s_4[side, to] = new_s
                else:
                    extra[q, side, :, lane(0)] = new_uv
                    extra[q, side, :, lane(1)] = new_pq
                    extra[q, side, :, lane(2)] = new_s

            return emit

        advance(states[3], [ROWS + r for r in pair], [into(side, r) for side, r in enumerate(pair)])
        for to in range(PEERS):
            fwd[q, to, :, lane(2)] = jnp.where(small, s_4[0, to], s_4[1, to])
        lax.fori_loop(0, PEERS - 1, lambda k, z: (fwd_copy(q, k).start(), z)[1], 0)
        got[q, lev] = fwd[q, lev]
        for side, r in enumerate(pair):
            step = lax.rem(r - lev - 1 + 2 * PEERS, PEERS)
            pl.when(r != lev)(lambda side=side, r=r, step=step: extra_copy(q, side, r, step).start())

            @pl.when(r == lev)
            def _(side=side):
                got[4, lev, :, 0:PIECE] = extra[q, side]

    def ret_copy(q, step):
        to = peer(step)
        return remote(ret.at[q, to], back.at[q, lev], ret_send.at[q, step], ret_recv.at[q, step], (lat, to))

    def last_copy(step):
        to, lanes = peer(step), pl.ds(0, 512)
        dst = back.at[4, lev, :, lanes]
        return remote(ret.at[4, to, :, lanes], dst, ret_send.at[4, step], ret_recv.at[4, step], (lat, to))

    def running(values):
        out, carry = [], None
        for v in values:
            for d in (1, 2, 4):
                v = v + jnp.where(sub >= d, pltpu.roll(v, d, 0), 0.0)
            if carry is not None:
                v = v + carry
            out.append(v)
            carry = v[7:8]
        return out

    def previous(values):
        out, carry = [], jnp.zeros((1, 128), jnp.float32)
        for v in values:
            out.append(jnp.where(sub == 0, carry, pltpu.roll(v, 1, 0)))
            carry = v[7:8]
        return out

    def gather(x, index):
        return jnp.take_along_axis(x, index, axis=0, mode="promise_in_bounds")

    def remap(q, side):
        first = side == 0
        row = jnp.where(q == 4, lev, jnp.where(first, 3 - q, 4 + q))
        t = jnp.where(q == 4, 8, lax.rem(lev - row + 2 * PEERS, PEERS))
        at = side * PIECE

        def split(n):
            xs = [got[q, p, :, pl.ds(pl.multiple_of(at + 128 * n, 128), 128)] for p in range(PEERS)]
            one = [jnp.where(small, xs[2 * i], flip(xs[2 * i + 1])) for i in range(4)]
            two = [jnp.where(small, flip(xs[2 * i]), xs[2 * i + 1]) for i in range(4)]
            return one, two

        zonal, meridional = split(0)
        temp, tracer = split(1)
        xs = [got[q, p, :, lane(2)] for p in range(PEERS)]
        layer = []
        for i in range(4):
            one = jnp.where(small, xs[2 * i], flip(xs[2 * i + 1]))
            two = jnp.where(small, flip(xs[2 * i]), xs[2 * i + 1])
            layer.append(jnp.exp(jnp.where(first, one, two)))
        lower = running(layer)
        upper = [x - y for x, y in zip(lower, layer)]
        bottom = lower[3][7:8]
        fields = (zonal, meridional, temp, tracer)
        before = []
        for f in fields:
            weighted = [x * y for x, y in zip(f, layer)]
            before.append([x - y for x, y in zip(running(weighted), weighted)])
        target = [bottom * bound[8 * i : 8 * i + 8, :] for i in range(4)]
        integral = [[] for _ in fields]
        ends = [lower[m][7:8] for m in range(3)]
        mids = [jnp.broadcast_to(lower[m][3:4], (8, 128)) for m in range(4)]
        for i in range(4):
            goal = target[i]
            past = [goal > e for e in ends]

            def pick(x):
                return jnp.where(past[2], x[3], jnp.where(past[1], x[2], jnp.where(past[0], x[1], x[0])))

            pos = jnp.where(pick(mids) < goal, 4, 0)
            pos = pos + jnp.where(pick([gather(x, pos + 1) for x in lower]) < goal, 2, 0)
            pos = pos + jnp.where(pick([gather(x, pos) for x in lower]) < goal, 1, 0)

            def here(xs):
                return pick([gather(x, pos) for x in xs])

            depth = goal - here(upper)
            for n, f in enumerate(fields):
                integral[n].append(here(before[n]) + depth * here(f))
        new_thick = [bottom * share[8 * i : 8 * i + 8, :] for i in range(4)]
        inverse = [1.0 / x for x in new_thick]
        remapped = [[(x - y) * z for x, y, z in zip(g, previous(g), inverse)] for g in integral]
        rise = [
            r * jnp.log((TOP_PRESSURE + x) / (TOP_PRESSURE + y))
            for r, x, y in zip(remapped[2], target, previous(target))
        ]
        geo = [None] * 4
        ground = surf[:, pl.ds(pl.multiple_of(t * 128, 128), 128)]
        carry = jnp.sum(jnp.where(sub == row, ground, 0.0), axis=0, keepdims=True)
        for i in (3, 2, 1, 0):
            x = rise[i]
            for d in (1, 2, 4):
                x = x + jnp.where(sub < 8 - d, pltpu.roll(x, 8 - d, 0), 0.0)
            geo[i] = x + carry
            carry = geo[i][0:1]
        for n, (one, two) in enumerate(((remapped[0], remapped[1]), (remapped[2], remapped[3]))):
            lanes = pl.ds(pl.multiple_of(at + 128 * n, 128), 128)
            for i in range(4):
                ret[q, 2 * i, :, lanes] = jnp.where(small, one[i], flip(two[i]))
                ret[q, 2 * i + 1, :, lanes] = jnp.where(small, flip(one[i]), two[i])
        mine = jnp.where(first, sub, 7 - sub) < 4
        floor = jnp.broadcast_to(bottom, (8, 128))
        for i in range(4):
            flipped = flip(geo[i])
            for p, x in ((2 * i, jnp.where(first, geo[i], flipped)), (2 * i + 1, jnp.where(first, flipped, geo[i]))):
                other = jnp.where(first, floor, ret[q, p, :, lane(2)])
                ret[q, p, :, lane(2)] = jnp.where(mine, x, other)
        bottoms[...] = jnp.where((sub == row) & (q < 4), floor, bottoms[...])

    def process(q):
        lax.fori_loop(0, PEERS - 1, lambda k, z: (fwd_copy(q, k).wait_recv(), z)[1], 0)
        lax.fori_loop(0, 2, lambda side, z: (remap(q, side), z)[1], 0)
        lax.fori_loop(0, PEERS - 1, lambda k, z: (ret_copy(q, k).start(), z)[1], 0)
        back[q, lev] = ret[q, lev]

    lax.fori_loop(5, 7, lambda m, z: (substep(1, 2 * m, 2 * m + 1), z)[1], 0)

    def front(h, depth):
        receive(0, h)
        receive(1, h)
        for n in range(1, min(depth, 3) + 1):
            substep(n, 8 + 2 * n - h, 15 - 2 * n + h)
        if depth == 4:
            release(h - 5)

    def passing(h):
        if relayed:
            pass_on(h)

    def late(m, carry):
        front(5 + 2 * m, 4)
        pl.when(m == 1)(lambda: process(0))
        front(6 + 2 * m, 4)
        pl.when(m == 1)(lambda: process(1))
        return carry

    passing(3)
    front(1, 2)
    passing(5)
    front(2, 2)
    passing(7)
    front(3, 3)
    front(4, 3)
    lax.fori_loop(0, 2, late, 0)
    lax.fori_loop(2, 4, lambda q, z: (process(q), z)[1], 0)
    lax.fori_loop(0, PEERS - 1, lambda k, z: (extra_copy(0, 0, 0, k).wait_recv(), z)[1], 0)
    remap(4, 0)
    for p in range(PEERS):
        ret[4, p, :, lane(3)] = bottoms[...]
    lax.fori_loop(0, PEERS - 1, lambda k, z: (last_copy(k).start(), z)[1], 0)
    back[4, lev, :, 0:512] = ret[4, lev, :, 0:512]

    for q in range(4):
        lax.fori_loop(0, PEERS - 1, lambda k, z, q=q: (ret_copy(q, k).wait(), z)[1], 0)
    lax.fori_loop(0, PEERS - 1, lambda k, z: (last_copy(k).wait(), z)[1], 0)

    def put(lanes, uv, pq, geo, bottom):
        for at, xs in ((0, uv), (64, pq)):
            for i, x in enumerate(transposed(xs)):
                out_ref[at + 8 * i : at + 8 * i + 8, lanes] = x
        for i, x in enumerate(transposed(geo)[:4]):
            out_geo_ref[8 * i : 8 * i + 8, lanes] = x
            out_thick_ref[8 * i : 8 * i + 8, lanes] = bottom * (splat[4 * lev + i] / total)

    def deliver(t, carry):
        uv, pq, geo = [], [], []
        bottom = jnp.zeros((8, 128), jnp.float32)
        for r in range(ROWS):
            owner, q, side = lax.rem(r + t, PEERS), max(3 - r, r - 4), r // 4
            uv.append(back[q, owner, :, side * PIECE : side * PIECE + 128])
            pq.append(back[q, owner, :, side * PIECE + 128 : side * PIECE + 256])
            x = back[q, owner, :, lane(2)]
            geo.append(flip(x) if side else x)
            bottom = jnp.where(sub == r, back[4, owner, :, lane(3)], bottom)
        put(pl.ds(pl.multiple_of(t * 128, 128), 128), uv, pq, geo, bottom)
        return carry

    lax.fori_loop(0, TILES - 1, deliver, 0)
    geo = [back[4, r, :, lane(2)] for r in range(ROWS)]
    bottom = jnp.zeros((8, 128), jnp.float32)
    for r in range(ROWS):
        bottom = jnp.where(sub == r, geo[r] if r >= 4 else flip(geo[r]), bottom)
    put(
        lane(8),
        [back[4, r, :, lane(0)] for r in range(ROWS)],
        [back[4, r, :, lane(1)] for r in range(ROWS)],
        geo,
        bottom,
    )

    for q in range(4):
        lax.fori_loop(0, PEERS - 1, lambda k, z, q=q: (fwd_copy(q, k).wait_send(), z)[1], 0)
    lax.fori_loop(0, PEERS - 1, lambda k, z: (extra_copy(0, 0, 0, k).wait_send(), z)[1], 0)
    for h in range(1, ROWS + 1):
        pl.when(has_south)(lambda h=h: to_south(h).wait_send())
        pl.when(has_north)(lambda h=h: to_north(h).wait_send())
    if relayed:
        for h in RELAYED:
            pl.when(relays_south)(lambda h=h: forward_south(h).wait_send())
            pl.when(relays_north)(lambda h=h: forward_north(h).wait_send())


def publish(remapped, thick, geo, out_ref, out_thick_ref, out_geo_ref, held, sem):
    pairs = [(remapped.at[pl.ds(32 * n, 32)], out_ref.at[pl.ds(32 * n, 32)]) for n in range(4)]
    pairs += [(thick, out_thick_ref), (geo, out_geo_ref)]
    reads = [pltpu.make_async_copy(src, held.at[n], sem.at[0, n]) for n, (src, _) in enumerate(pairs)]
    writes = [pltpu.make_async_copy(held.at[n], dst, sem.at[1, n]) for n, (_, dst) in enumerate(pairs)]
    for copy in reads:
        copy.start()
    for read, write in zip(reads, writes):
        read.wait()
        write.start()
    for copy in writes:
        copy.wait()


def shards(lat_size, velocity, potential_temp, tracer, thickness, surface_height, level_fractions):
    hbm = pl.BlockSpec(memory_space=pltpu.HBM)
    f32 = jnp.float32
    out_shape = (
        jax.ShapeDtypeStruct((128, LON), f32),
        jax.ShapeDtypeStruct((32, LON), f32),
        jax.ShapeDtypeStruct((32, LON), f32),
    )
    results = pl.pallas_call(
        functools.partial(kernel, lat_size),
        out_shape=out_shape,
        in_specs=[hbm] * 6,
        out_specs=(pl.BlockSpec(memory_space=pltpu.VMEM),) * 3,
        scratch_shapes=[
            pltpu.SMEM((32,), f32),
            pltpu.VMEM((160, LON), f32),
            pltpu.VMEM((3 * ROWS, 8, ROW), f32),
            *[pltpu.VMEM((3 * ROWS, 8, LON), f32)] * 10,
            pltpu.VMEM((3 * ROWS, 8, 128), f32),
            pltpu.VMEM((32, 128), f32),
            pltpu.VMEM((32, 128), f32),
            pltpu.VMEM((32, 8, 128), f32),
            pltpu.VMEM((ROWS, LON), f32),
            pltpu.VMEM((len(RELAYED), 8, ROW), f32),
            pltpu.VMEM((4, PEERS, 8, PAIR), f32),
            pltpu.VMEM((4, 2, 8, PIECE), f32),
            pltpu.VMEM((2, PEERS, 8, 128), f32),
            pltpu.VMEM((5, PEERS, 8, PAIR), f32),
            pltpu.VMEM((5, PEERS, 8, PAIR), f32),
            pltpu.VMEM((8, 128), f32),
            pltpu.VMEM((5, PEERS, 8, PAIR), f32),
            pltpu.SemaphoreType.DMA((6,)),
            pltpu.SemaphoreType.DMA((2, ROWS)),
            pltpu.SemaphoreType.DMA((2, ROWS)),
            pltpu.SemaphoreType.DMA((len(RELAYED),)),
            pltpu.SemaphoreType.DMA((len(RELAYED),)),
            pltpu.SemaphoreType.DMA((5, PEERS - 1)),
            pltpu.SemaphoreType.DMA((5, PEERS - 1)),
            pltpu.SemaphoreType.DMA((5, PEERS - 1)),
            pltpu.SemaphoreType.DMA((5, PEERS - 1)),
        ],
        compiler_params=pltpu.CompilerParams(
            collective_id=0, has_side_effects=True, vmem_limit_bytes=60 * 2**20
        ),
        cost_estimate=pl.CostEstimate(flops=10**8, bytes_accessed=2 * 10**6, transcendentals=10**6),
    )(
        velocity.reshape(64, LON),
        potential_temp.reshape(32, LON),
        tracer.reshape(32, LON),
        thickness.reshape(32, LON),
        surface_height,
        level_fractions,
    )
    remapped, new_thickness, geopotential = pl.pallas_call(
        publish,
        out_shape=out_shape,
        in_specs=[hbm] * 3,
        out_specs=(hbm,) * 3,
        scratch_shapes=[pltpu.VMEM((6, 32, LON), f32), pltpu.SemaphoreType.DMA((2, 6))],
        compiler_params=pltpu.CompilerParams(vmem_limit_bytes=60 * 2**20),
        cost_estimate=pl.CostEstimate(flops=0, bytes_accessed=2 * 10**6, transcendentals=0),
    )(*results)
    return (
        remapped.reshape(4, 4, ROWS, LON),
        new_thickness.reshape(4, ROWS, LON),
        geopotential.reshape(4, ROWS, LON),
    )


def solution(mesh):
    return jax.shard_map(
        functools.partial(shards, mesh.shape["lat"]),
        mesh=mesh,
        in_specs=(
            P(None, "lev", "lat", None),
            P("lev", "lat", None),
            P("lev", "lat", None),
            P("lev", "lat", None),
            P("lat", None),
            P(),
        ),
        out_specs=(P(None, "lev", "lat", None), P("lev", "lat", None), P("lev", "lat", None)),
        check_vma=False,
    )
```

```python
import functools
import math

import jax
import jax.numpy as jnp
from jax import lax
from jax.experimental import pallas as pl
from jax.experimental.pallas import tpu as pltpu
from jax.sharding import PartitionSpec as P

MESH = pl.DeviceIdType.MESH
SUBSTEPS = 4
ADVECT = 0.3 / 12.0
PRESS = 0.15 / 12.0
ROTATION_RATE = 0.3
TOP_PRESSURE = 1.0

ROWS = 8
LON = 1152
TILES = 9
ROW = 2 * LON + 640
PIECE = 384
PAIR = 640
PEERS = 8
RING = 8
RELAYED = (3, 5, 7)


def flip(x):
    return pltpu.roll(x, 4, 0)


def transposed(xs):
    sub = lax.broadcasted_iota(jnp.int32, (8, 128), 0)
    for d in (4, 2, 1):
        ys = list(xs)
        for i in range(8):
            if not i & d:
                ys[i] = jnp.where(sub & d == 0, xs[i], pltpu.roll(xs[i + d], d, 0))
                ys[i + d] = jnp.where(sub & d == 0, pltpu.roll(xs[i], 8 - d, 0), xs[i + d])
        xs = ys
    return xs


def kernel(
    lat_size,
    vel_ref, temp_ref, tracer_ref, thick_ref, surf_ref, frac_ref,
    back,
    frac, band, rows, s_0, uv_1, pq_1, s_1, uv_2, pq_2, s_2, uv_3, pq_3, s_3, turn, bound, share, surf,
    relay, fwd, extra, s_4, got, ret, bottoms, bases,
    local_sem, halo_send, halo_recv, relay_send, relay_recv, fwd_send, fwd_recv, ret_send, ret_recv, own_sem,
):
    lat, lev = lax.axis_index("lat"), lax.axis_index("lev")
    relayed = lat_size % RING == 0 and lat_size > RING

    def band_at(offset):
        return lax.rem(lat + offset + lat_size, lat_size)

    def lane(t):
        return slice(128 * t, 128 * t + 128)

    parts = ((vel_ref, 0, 64), (temp_ref, 64, 32), (tracer_ref, 96, 32), (thick_ref, 128, 32))
    own = [
        pltpu.make_async_copy(ref, band.at[pl.ds(at, size)], local_sem.at[n])
        for n, (ref, at, size) in enumerate(parts)
    ]
    later = [
        pltpu.make_async_copy(surf_ref, surf, local_sem.at[4]),
        pltpu.make_async_copy(frac_ref, frac, local_sem.at[5]),
    ]
    for copy in own + later:
        copy.start()

    has_north, has_south = lat > 0, lat < lat_size - 1
    before_step = lax.rem(lat, RING) == RING - 1
    after_step = lax.rem(lat, RING) == 0
    beside = band_at(jnp.where(before_step, 1 - RING, RING - 1))
    ahead, behind = lat + RING < lat_size, lat >= RING
    relays_south = after_step & ahead
    relays_north = before_step & behind

    barrier = pltpu.get_barrier_semaphore()

    def greet(row):
        pl.semaphore_signal(barrier, inc=1, device_id=(row, lev), device_id_type=MESH)

    def peer(step):
        return lax.rem(lev + 1 + step, PEERS)

    pl.when(has_north)(lambda: greet(band_at(-1)))
    pl.when(has_south)(lambda: greet(band_at(1)))
    for step in range(PEERS - 1):
        pl.semaphore_signal(barrier, inc=1, device_id=(lat, peer(step)), device_id_type=MESH)
    guests = PEERS - 1 + jnp.where(has_north, 1, 0) + jnp.where(has_south, 1, 0)
    if relayed:

        @pl.when(before_step | after_step)
        def _():
            greet(beside)
            pl.when(ahead)(lambda: greet(band_at(RING)))
            pl.when(behind)(lambda: greet(band_at(-RING)))

        more = 1 + jnp.where(ahead, 1, 0) + jnp.where(behind, 1, 0)
        guests = guests + jnp.where(before_step | after_step, more, 0)

    sub = lax.broadcasted_iota(jnp.int32, (8, 128), 0)
    lanes_in = lax.broadcasted_iota(jnp.int32, (8, 128), 1)
    small = sub < 4

    for copy in own:
        copy.wait()

    def unpack(t, carry):
        at = pl.multiple_of(t * 128, 128)
        for start, n in ((0, 0), (LON, 64)):
            xs = [band[n + 8 * i : n + 8 * i + 8, pl.ds(at, 128)] for i in range(8)]
            for r, x in enumerate(transposed(xs)):
                rows[ROWS + r, :, pl.ds(start + at, 128)] = x
        xs = [jnp.log(band[128 + 8 * i : 136 + 8 * i, pl.ds(at, 128)]) for i in range(4)]
        for r, x in enumerate(transposed(xs + xs)):
            s_0[ROWS + r, :, pl.ds(at, 128)] = x
        return carry

    lax.fori_loop(0, TILES, unpack, 0)

    def fold(r, carry):
        j = ROWS + r
        for t in range(4):
            x = jnp.where(small, s_0[j, :, lane(t)], s_0[j, :, lane(t + 5)])
            rows[j, :, 2 * LON + 128 * t : 2 * LON + 128 * (t + 1)] = x
        rows[j, :, 2 * LON + 512 :] = s_0[j, :, lane(4)]
        return carry

    lax.fori_loop(0, ROWS, fold, 0)

    pl.semaphore_wait(barrier, guests)

    def remote(src, dst, send, recv, to):
        return pltpu.make_async_remote_copy(
            src_ref=src, dst_ref=dst, send_sem=send, recv_sem=recv, device_id=to, device_id_type=MESH
        )

    def to_south(h, src=None, row=None, send=None):
        return remote(
            rows.at[2 * ROWS - h] if src is None else src,
            rows.at[ROWS - h],
            halo_send.at[0, h - 1] if send is None else send,
            halo_recv.at[0, h - 1],
            (band_at(1) if row is None else row, lev),
        )

    def to_north(h, src=None, row=None, send=None):
        return remote(
            rows.at[ROWS - 1 + h] if src is None else src,
            rows.at[2 * ROWS - 1 + h],
            halo_send.at[1, h - 1] if send is None else send,
            halo_recv.at[1, h - 1],
            (band_at(-1) if row is None else row, lev),
        )

    def to_relay(way, h):
        n = RELAYED.index(h)
        src = rows.at[2 * ROWS - h] if way == 0 else rows.at[ROWS - 1 + h]
        return remote(src, relay.at[n], halo_send.at[way, h - 1], relay_recv.at[n], (beside, lev))

    for h in range(1, ROWS + 1):
        if relayed and h in RELAYED:
            pl.when(has_south & before_step)(lambda h=h: to_relay(0, h).start())
            pl.when(has_south & jnp.logical_not(before_step))(lambda h=h: to_south(h).start())
            pl.when(has_north & after_step)(lambda h=h: to_relay(1, h).start())
            pl.when(has_north & jnp.logical_not(after_step))(lambda h=h: to_north(h).start())
        else:
            pl.when(has_south)(lambda h=h: to_south(h).start())
            pl.when(has_north)(lambda h=h: to_north(h).start())

    def forward_south(h):
        return to_south(h, relay.at[RELAYED.index(h)], band_at(RING), relay_send.at[RELAYED.index(h)])

    def forward_north(h):
        return to_north(h, relay.at[RELAYED.index(h)], band_at(-RING), relay_send.at[RELAYED.index(h)])

    def pass_on(h):
        @pl.when(relays_south)
        def _():
            to_relay(0, h).wait_recv()
            forward_south(h).start()

        @pl.when(relays_north)
        def _():
            to_relay(1, h).wait_recv()
            forward_north(h).start()

    for copy in later:
        copy.wait()
    total = jnp.float32(0.0)
    for k in range(4 * PEERS):
        total = total + frac[k]
        share[k, :] = jnp.full((128,), frac[k], jnp.float32)
        bound[k, :] = jnp.full((128,), total, jnp.float32)
    share[...] = share[...] / total
    bound[...] = bound[...] / total
    bottoms[...] = jnp.zeros((8, 128), jnp.float32)
    bases[...] = jnp.zeros((PEERS, 8, 128), jnp.float32)
    row_of = lax.broadcasted_iota(jnp.int32, (3 * ROWS, 8, 128), 0) + (lat - 1) * ROWS
    angle = -0.5 * math.pi + (row_of.astype(jnp.float32) + 0.5) * (math.pi / (lat_size * ROWS))
    sign = jnp.where(lax.broadcasted_iota(jnp.int32, (3 * ROWS, 8, 128), 1) < 4, ROTATION_RATE, -ROTATION_RATE)
    turn[...] = sign * jnp.sin(angle)

    def inside(j):
        row = (lat - 1) * ROWS + j
        return jnp.where((row >= 0) & (row < lat_size * ROWS), 1.0, 0.0).astype(jnp.float32)

    def advance(state, js, emits):
        (uv_ref, _), (pq_ref, pq_at), (s_ref, _) = state
        fields = ((uv_ref, 0), (pq_ref, pq_at), (s_ref, 0))

        def line(j, emit):
            spin = turn[j]

            def load(n, row, t):
                ref, at = fields[n]
                return ref[row, :, at + 128 * t : at + 128 * (t + 1)]

            here, rolled = {}, {}

            def value(n, t):
                if (n, t) not in here:
                    here[n, t] = load(n, j, t)
                return here[n, t]

            def roll(n, t, k):
                t = t % TILES
                if (n, t, k) not in rolled:
                    rolled[n, t, k] = pltpu.roll(value(n, t), k, 1)
                return rolled[n, t, k]

            def east(n, t):
                one = jnp.where(lanes_in < 127, roll(n, t, 127), roll(n, t + 1, 127)) - jnp.where(
                    lanes_in < 1, roll(n, t - 1, 1), roll(n, t, 1)
                )
                two = jnp.where(lanes_in < 126, roll(n, t, 126), roll(n, t + 1, 126)) - jnp.where(
                    lanes_in < 2, roll(n, t - 1, 2), roll(n, t, 2)
                )
                return 8.0 * one - two

            def up(n, t):
                return 8.0 * (load(n, j + 1, t) - load(n, j - 1, t)) - (load(n, j + 2, t) - load(n, j - 2, t))

            def step(t):
                uv, pq, s = (value(n, t) for n in range(3))
                turned = flip(uv)
                eastward = jnp.where(small, uv, turned) * ADVECT
                northward = jnp.where(small, turned, uv) * ADVECT
                uv_east, uv_up = east(0, t), up(0, t)
                s_east, s_up = east(2, t), up(2, t)
                new_pq = pq - eastward * east(1, t) - northward * up(1, t)
                push = PRESS * jnp.where(small, s_east, s_up)
                new_uv = uv - eastward * uv_east - northward * uv_up - push + spin * turned
                spread = jnp.where(small, uv_east, uv_up)
                new_s = s - eastward * s_east - northward * s_up - ADVECT * (spread + flip(spread))
                emit(t, new_uv, new_pq, new_s)

            return step

        steps = [line(j, emit) for j, emit in zip(js, emits)]
        for t in range(TILES):
            for step in steps:
                step(t)

    states = (
        ((rows, 0), (rows, LON), (s_0, 0)),
        ((uv_1, 0), (pq_1, 0), (s_1, 0)),
        ((uv_2, 0), (pq_2, 0), (s_2, 0)),
        ((uv_3, 0), (pq_3, 0), (s_3, 0)),
    )

    def substep(n, *js):
        dst = states[n]

        def into(j):
            keep = inside(j)

            def emit(t, new_uv, new_pq, new_s):
                dst[0][0][j, :, lane(t)] = new_uv * keep
                dst[1][0][j, :, lane(t)] = new_pq
                dst[2][0][j, :, lane(t)] = new_s * keep

            return emit

        advance(states[n - 1], js, [into(j) for j in js])

    def receive(way, h):
        j = ROWS - h if way == 0 else 2 * ROWS - 1 + h
        there = has_north if way == 0 else has_south
        pl.when(there)(lambda: (to_south(h) if way == 0 else to_north(h)).wait_recv())

        @pl.when(jnp.logical_not(there))
        def _():
            rows[j] = jnp.zeros((8, ROW), jnp.float32)

        for t in range(5):
            x = rows[j, :, 2 * LON + 128 * t : 2 * LON + 128 * (t + 1)]
            y = flip(x)
            s_0[j, :, lane(t)] = jnp.where(small, x, y)
            if t < 4:
                s_0[j, :, lane(t + 5)] = jnp.where(small, y, x)

    def fwd_copy(q, step):
        to = peer(step)
        return remote(fwd.at[q, to], got.at[q, lev], fwd_send.at[q, step], fwd_recv.at[q, step], (lat, to))

    def extra_copy(q, side, to, step):
        dst = got.at[4, lev, :, pl.ds(0, PIECE)]
        return remote(extra.at[q, side], dst, fwd_send.at[4, step], fwd_recv.at[4, step], (lat, to))

    def release(q):
        pair = (3 - q, 4 + q)

        def into(side, r):
            at = side * PIECE

            def emit(t, new_uv, new_pq, new_s):
                if t < 8:
                    to = lax.rem(r + t, PEERS)
                    fwd[q, to, :, at : at + 128] = new_uv
                    fwd[q, to, :, at + 128 : at + 256] = new_pq
                    s_4[side, to] = new_s
                else:
                    extra[q, side, :, lane(0)] = new_uv
                    extra[q, side, :, lane(1)] = new_pq
                    extra[q, side, :, lane(2)] = new_s

            return emit

        advance(states[3], [ROWS + r for r in pair], [into(side, r) for side, r in enumerate(pair)])
        for to in range(PEERS):
            fwd[q, to, :, lane(2)] = jnp.where(small, s_4[0, to], s_4[1, to])
        lax.fori_loop(0, PEERS - 1, lambda k, z: (fwd_copy(q, k).start(), z)[1], 0)
        got[q, lev] = fwd[q, lev]
        for side, r in enumerate(pair):
            step = lax.rem(r - lev - 1 + 2 * PEERS, PEERS)
            pl.when(r != lev)(lambda side=side, r=r, step=step: extra_copy(q, side, r, step).start())

            @pl.when(r == lev)
            def _(side=side):
                got[4, lev, :, 0:PIECE] = extra[q, side]

    def ret_copy(q, step):
        to, lanes = peer(step), pl.ds(0, PAIR if q is None else 512)
        n = 4 if q is None else q
        dst = back.at[n, lev, :, lanes]
        return remote(ret.at[n, to, :, lanes], dst, ret_send.at[n, step], ret_recv.at[n, step], (lat, to))

    def own_copy(q):
        return pltpu.make_async_copy(ret.at[q, lev], back.at[q, lev], own_sem.at[q])

    def running(values):
        out, carry = [], None
        for v in values:
            for d in (1, 2, 4):
                v = v + jnp.where(sub >= d, pltpu.roll(v, d, 0), 0.0)
            if carry is not None:
                v = v + carry
            out.append(v)
            carry = v[7:8]
        return out

    def previous(values):
        out, carry = [], jnp.zeros((1, 128), jnp.float32)
        for v in values:
            out.append(jnp.where(sub == 0, carry, pltpu.roll(v, 1, 0)))
            carry = v[7:8]
        return out

    def gather(x, index):
        return jnp.take_along_axis(x, index, axis=0, mode="promise_in_bounds")

    def remap(q, side):
        first = side == 0
        row = jnp.where(q == 4, lev, jnp.where(first, 3 - q, 4 + q))
        t = jnp.where(q == 4, 8, lax.rem(lev - row + 2 * PEERS, PEERS))
        at, ret_at = side * PIECE, side * 256

        def split(n):
            xs = [got[q, p, :, pl.ds(pl.multiple_of(at + 128 * n, 128), 128)] for p in range(PEERS)]
            one = [jnp.where(small, xs[2 * i], flip(xs[2 * i + 1])) for i in range(4)]
            two = [jnp.where(small, flip(xs[2 * i]), xs[2 * i + 1]) for i in range(4)]
            return one, two

        zonal, meridional = split(0)
        temp, tracer = split(1)
        xs = [got[q, p, :, lane(2)] for p in range(PEERS)]
        layer = []
        for i in range(4):
            one = jnp.where(small, xs[2 * i], flip(xs[2 * i + 1]))
            two = jnp.where(small, flip(xs[2 * i]), xs[2 * i + 1])
            layer.append(jnp.exp(jnp.where(first, one, two)))
        lower = running(layer)
        upper = [x - y for x, y in zip(lower, layer)]
        bottom = lower[3][7:8]
        fields = (zonal, meridional, temp, tracer)
        before = []
        for f in fields:
            weighted = [x * y for x, y in zip(f, layer)]
            before.append([x - y for x, y in zip(running(weighted), weighted)])
        target = [bottom * bound[8 * i : 8 * i + 8, :] for i in range(4)]
        integral = [[] for _ in fields]
        ends = [lower[m][7:8] for m in range(3)]
        mids = [jnp.broadcast_to(lower[m][3:4], (8, 128)) for m in range(4)]
        for i in range(4):
            goal = target[i]
            past = [goal > e for e in ends]

            def pick(x):
                return jnp.where(past[2], x[3], jnp.where(past[1], x[2], jnp.where(past[0], x[1], x[0])))

            pos = jnp.where(pick(mids) < goal, 4, 0)
            pos = pos + jnp.where(pick([gather(x, pos + 1) for x in lower]) < goal, 2, 0)
            pos = pos + jnp.where(pick([gather(x, pos) for x in lower]) < goal, 1, 0)

            def here(xs):
                return pick([gather(x, pos) for x in xs])

            depth = goal - here(upper)
            for n, f in enumerate(fields):
                integral[n].append(here(before[n]) + depth * here(f))
        new_thick = [bottom * share[8 * i : 8 * i + 8, :] for i in range(4)]
        inverse = [1.0 / x for x in new_thick]
        remapped = [[(x - y) * z for x, y, z in zip(g, previous(g), inverse)] for g in integral]
        rise = [
            r * jnp.log((TOP_PRESSURE + x) / (TOP_PRESSURE + y))
            for r, x, y in zip(remapped[2], target, previous(target))
        ]
        geo = [None] * 4
        ground = surf[:, pl.ds(pl.multiple_of(t * 128, 128), 128)]
        ground_row = jnp.sum(jnp.where(sub == row, ground, 0.0), axis=0, keepdims=True)
        carry = ground_row
        for i in (3, 2, 1, 0):
            x = rise[i]
            for d in (1, 2, 4):
                x = x + jnp.where(sub < 8 - d, pltpu.roll(x, 8 - d, 0), 0.0)
            geo[i] = x + carry
            carry = geo[i][0:1]
        for n, (one, two) in enumerate(((remapped[0], remapped[1]), (remapped[2], remapped[3]))):
            lanes = pl.ds(pl.multiple_of(ret_at + 128 * n, 128), 128)
            for i in range(4):
                ret[q, 2 * i, :, lanes] = jnp.where(small, one[i], flip(two[i]))
                ret[q, 2 * i + 1, :, lanes] = jnp.where(small, flip(one[i]), two[i])
        floor = jnp.broadcast_to(bottom, (8, 128))
        below = [x for i in range(4) for x in (geo[i][4:5], geo[i + 1][0:1] if i < 3 else ground_row)]

        @pl.when(q < 4)
        def _():
            bottoms[...] = jnp.where(sub == row, floor, bottoms[...])
            for p in range(PEERS):
                bases[p] = jnp.where(sub == row, below[p], bases[p])

        @pl.when(q == 4)
        def _():
            for p in range(PEERS):
                ret[4, p, :, lane(2)] = jnp.where(small, floor, below[p])
                ret[4, p, :, lane(3)] = bottoms[...]
                ret[4, p, :, lane(4)] = bases[p]

    def process(q):
        lax.fori_loop(0, PEERS - 1, lambda k, z: (fwd_copy(q, k).wait_recv(), z)[1], 0)
        lax.fori_loop(0, 2, lambda side, z: (remap(q, side), z)[1], 0)
        lax.fori_loop(0, PEERS - 1, lambda k, z: (ret_copy(q, k).start(), z)[1], 0)
        own_copy(q).start()

    lax.fori_loop(5, 7, lambda m, z: (substep(1, 2 * m, 2 * m + 1), z)[1], 0)

    def front(h, depth):
        receive(0, h)
        receive(1, h)
        for n in range(1, min(depth, 3) + 1):
            substep(n, 8 + 2 * n - h, 15 - 2 * n + h)
        if depth == 4:
            release(h - 5)

    def passing(h):
        if relayed:
            pass_on(h)

    def late(m, carry):
        front(5 + 2 * m, 4)
        pl.when(m == 1)(lambda: process(0))
        front(6 + 2 * m, 4)
        pl.when(m == 1)(lambda: process(1))
        return carry

    passing(3)
    front(1, 2)
    passing(5)
    front(2, 2)
    passing(7)
    front(3, 3)
    front(4, 3)
    lax.fori_loop(0, 2, late, 0)
    lax.fori_loop(2, 4, lambda q, z: (process(q), z)[1], 0)
    lax.fori_loop(0, PEERS - 1, lambda k, z: (extra_copy(0, 0, 0, k).wait_recv(), z)[1], 0)
    remap(4, 0)
    lax.fori_loop(0, PEERS - 1, lambda k, z: (ret_copy(None, k).start(), z)[1], 0)
    own_copy(4).start()
    for q in (0, 1, 2, 3, None):
        lax.fori_loop(0, PEERS - 1, lambda k, z, q=q: (ret_copy(q, k).wait(), z)[1], 0)
    for q in range(5):
        own_copy(q).wait()
    for q in range(4):
        lax.fori_loop(0, PEERS - 1, lambda k, z, q=q: (fwd_copy(q, k).wait_send(), z)[1], 0)
    lax.fori_loop(0, PEERS - 1, lambda k, z: (extra_copy(0, 0, 0, k).wait_send(), z)[1], 0)
    for h in range(1, ROWS + 1):
        pl.when(has_south)(lambda h=h: to_south(h).wait_send())
        pl.when(has_north)(lambda h=h: to_north(h).wait_send())
    if relayed:
        for h in RELAYED:
            pl.when(relays_south)(lambda h=h: forward_south(h).wait_send())
            pl.when(relays_north)(lambda h=h: forward_north(h).wait_send())


def publish(back, frac_ref, out_ref, out_thick_ref, out_geo_ref, frac, held, out, thick, heights, read_sem, write_sem):
    lev = lax.axis_index("lev")
    fractions = pltpu.make_async_copy(frac_ref, frac, read_sem.at[5])
    fractions.start()
    reads = [pltpu.make_async_copy(back.at[n], held.at[n], read_sem.at[n]) for n in range(5)]
    for copy in reads:
        copy.start()
    fractions.wait()

    total, above = jnp.float32(0.0), [jnp.float32(0.0)] * 5
    for k in range(4 * PEERS):
        for i in range(5):
            above[i] = jnp.where(k == 4 * lev + i, total, above[i])
        total = total + frac[k]
    above[4] = jnp.where(lev == PEERS - 1, total, above[4])
    bounds = [jnp.full((8, 128), x, jnp.float32) / total for x in above]
    shares = [jnp.full((8, 128), frac[4 * lev + i], jnp.float32) / total for i in range(4)]
    sub = lax.broadcasted_iota(jnp.int32, (8, 128), 0)

    def lane(t):
        return slice(128 * t, 128 * t + 128)

    def put(t, uv, pq, bottom, base):
        lanes = lane(t)
        uv, pq = transposed(uv), transposed(pq)
        for i in range(8):
            out[8 * i : 8 * i + 8, lanes] = uv[i]
            out[64 + 8 * i : 72 + 8 * i, lanes] = pq[i]
        pressure = [TOP_PRESSURE + bottom * x for x in bounds]
        height = base
        for i in (3, 2, 1, 0):
            height = height + pq[i] * jnp.log(pressure[i + 1] / pressure[i])
            heights[8 * i : 8 * i + 8, lanes] = height
            thick[8 * i : 8 * i + 8, lanes] = bottom * shares[i]

    def deliver(t):
        uv, pq = [], []
        bottom = base = jnp.zeros((8, 128), jnp.float32)
        for r in range(ROWS):
            owner, q, side = (r + t) % PEERS, max(3 - r, r - 4), r // 4
            uv.append(held[q, owner, :, lane(2 * side)])
            pq.append(held[q, owner, :, lane(2 * side + 1)])
            bottom = jnp.where(sub == r, held[4, owner, :, lane(3)], bottom)
            base = jnp.where(sub == r, held[4, owner, :, lane(4)], base)
        put(t, uv, pq, bottom, base)

    def deliver_last():
        bottom = base = jnp.zeros((8, 128), jnp.float32)
        for r in range(ROWS):
            x = held[4, r, :, lane(2)]
            bottom = jnp.where(sub == r, flip(x) if r >= 4 else x, bottom)
            base = jnp.where(sub == r, x if r >= 4 else flip(x), base)
        put(8, [held[4, r, :, lane(0)] for r in range(ROWS)], [held[4, r, :, lane(1)] for r in range(ROWS)], bottom, base)

    for copy in reads:
        copy.wait()
    writes = []
    for c in range(3):
        for t in range(3 * c, min(3 * c + 3, TILES - 1)):
            deliver(t)
        if c == 2:
            deliver_last()
        lanes = pl.ds(384 * c, 384)
        for n, (src, dst) in enumerate(((out, out_ref), (thick, out_thick_ref), (heights, out_geo_ref))):
            writes.append(pltpu.make_async_copy(src.at[:, lanes], dst.at[:, lanes], write_sem.at[c, n]))
            writes[-1].start()
    for copy in writes:
        copy.wait()


def shards(lat_size, velocity, potential_temp, tracer, thickness, surface_height, level_fractions):
    hbm = pl.BlockSpec(memory_space=pltpu.HBM)
    f32 = jnp.float32
    out_shape = (
        jax.ShapeDtypeStruct((128, LON), f32),
        jax.ShapeDtypeStruct((32, LON), f32),
        jax.ShapeDtypeStruct((32, LON), f32),
    )
    returned = pl.pallas_call(
        functools.partial(kernel, lat_size),
        out_shape=jax.ShapeDtypeStruct((5, PEERS, 8, PAIR), f32),
        in_specs=[hbm] * 6,
        out_specs=hbm,
        scratch_shapes=[
            pltpu.SMEM((32,), f32),
            pltpu.VMEM((160, LON), f32),
            pltpu.VMEM((3 * ROWS, 8, ROW), f32),
            *[pltpu.VMEM((3 * ROWS, 8, LON), f32)] * 10,
            pltpu.VMEM((3 * ROWS, 8, 128), f32),
            pltpu.VMEM((32, 128), f32),
            pltpu.VMEM((32, 128), f32),
            pltpu.VMEM((ROWS, LON), f32),
            pltpu.VMEM((len(RELAYED), 8, ROW), f32),
            pltpu.VMEM((4, PEERS, 8, PAIR), f32),
            pltpu.VMEM((4, 2, 8, PIECE), f32),
            pltpu.VMEM((2, PEERS, 8, 128), f32),
            pltpu.VMEM((5, PEERS, 8, PAIR), f32),
            pltpu.VMEM((5, PEERS, 8, PAIR), f32),
            pltpu.VMEM((8, 128), f32),
            pltpu.VMEM((PEERS, 8, 128), f32),
            pltpu.SemaphoreType.DMA((6,)),
            pltpu.SemaphoreType.DMA((2, ROWS)),
            pltpu.SemaphoreType.DMA((2, ROWS)),
            pltpu.SemaphoreType.DMA((len(RELAYED),)),
            pltpu.SemaphoreType.DMA((len(RELAYED),)),
            pltpu.SemaphoreType.DMA((5, PEERS - 1)),
            pltpu.SemaphoreType.DMA((5, PEERS - 1)),
            pltpu.SemaphoreType.DMA((5, PEERS - 1)),
            pltpu.SemaphoreType.DMA((5, PEERS - 1)),
            pltpu.SemaphoreType.DMA((5,)),
        ],
        compiler_params=pltpu.CompilerParams(
            collective_id=0, has_side_effects=True, vmem_limit_bytes=60 * 2**20
        ),
        cost_estimate=pl.CostEstimate(flops=10**8, bytes_accessed=2 * 10**6, transcendentals=10**6),
    )(
        velocity.reshape(64, LON),
        potential_temp.reshape(32, LON),
        tracer.reshape(32, LON),
        thickness.reshape(32, LON),
        surface_height,
        level_fractions,
    )
    remapped, new_thickness, geopotential = pl.pallas_call(
        publish,
        out_shape=out_shape,
        in_specs=[hbm] * 2,
        out_specs=(hbm,) * 3,
        scratch_shapes=[
            pltpu.SMEM((32,), f32),
            pltpu.VMEM((5, PEERS, 8, PAIR), f32),
            pltpu.VMEM((128, LON), f32),
            pltpu.VMEM((32, LON), f32),
            pltpu.VMEM((32, LON), f32),
            pltpu.SemaphoreType.DMA((6,)),
            pltpu.SemaphoreType.DMA((3, 3)),
        ],
        compiler_params=pltpu.CompilerParams(vmem_limit_bytes=60 * 2**20),
        cost_estimate=pl.CostEstimate(flops=0, bytes_accessed=2 * 10**6, transcendentals=0),
    )(returned, level_fractions)
    return (
        remapped.reshape(4, 4, ROWS, LON),
        new_thickness.reshape(4, ROWS, LON),
        geopotential.reshape(4, ROWS, LON),
    )


def solution(mesh):
    return jax.shard_map(
        functools.partial(shards, mesh.shape["lat"]),
        mesh=mesh,
        in_specs=(
            P(None, "lev", "lat", None),
            P("lev", "lat", None),
            P("lev", "lat", None),
            P("lev", "lat", None),
            P("lat", None),
            P(),
        ),
        out_specs=(P(None, "lev", "lat", None), P("lev", "lat", None), P("lev", "lat", None)),
        check_vma=False,
    )
```

```python
import functools
import math

import jax
import jax.numpy as jnp
from jax import lax
from jax.experimental import pallas as pl
from jax.experimental.pallas import tpu as pltpu
from jax.sharding import PartitionSpec as P

MESH = pl.DeviceIdType.MESH
SUBSTEPS = 4
ADVECT = 0.3 / 12.0
PRESS = 0.15 / 12.0
ROTATION_RATE = 0.3
TOP_PRESSURE = 1.0

ROWS = 8
LON = 1152
TILES = 9
ROW = 2 * LON + 640
PIECE = 384
PAIR = 640
PEERS = 8
RING = 8
RELAYED = (3, 5, 7)


def flip(x):
    return pltpu.roll(x, 4, 0)


def transposed(xs):
    sub = lax.broadcasted_iota(jnp.int32, (8, 128), 0)
    for d in (4, 2, 1):
        ys = list(xs)
        for i in range(8):
            if not i & d:
                ys[i] = jnp.where(sub & d == 0, xs[i], pltpu.roll(xs[i + d], d, 0))
                ys[i + d] = jnp.where(sub & d == 0, pltpu.roll(xs[i], 8 - d, 0), xs[i + d])
        xs = ys
    return xs


def kernel(
    lat_size,
    vel_ref, temp_ref, tracer_ref, thick_ref, surf_ref, frac_ref,
    back,
    frac, band, rows, s_0, uv_1, pq_1, s_1, uv_2, pq_2, s_2, uv_3, pq_3, s_3, turn, bound, share, surf,
    relay, fwd, extra, s_4, got, ret, bottoms, bases,
    local_sem, halo_send, halo_recv, relay_send, relay_recv, fwd_send, fwd_recv, ret_send, ret_recv, own_sem,
):
    lat, lev = lax.axis_index("lat"), lax.axis_index("lev")
    relayed = lat_size % RING == 0 and lat_size > RING

    def band_at(offset):
        return lax.rem(lat + offset + lat_size, lat_size)

    def lane(t):
        return slice(128 * t, 128 * t + 128)

    parts = ((vel_ref, 0, 64), (temp_ref, 64, 32), (tracer_ref, 96, 32), (thick_ref, 128, 32))
    own = [
        pltpu.make_async_copy(ref, band.at[pl.ds(at, size)], local_sem.at[n])
        for n, (ref, at, size) in enumerate(parts)
    ]
    later = [
        pltpu.make_async_copy(surf_ref, surf, local_sem.at[4]),
        pltpu.make_async_copy(frac_ref, frac, local_sem.at[5]),
    ]
    for copy in own + later:
        copy.start()

    has_north, has_south = lat > 0, lat < lat_size - 1
    before_step = lax.rem(lat, RING) == RING - 1
    after_step = lax.rem(lat, RING) == 0
    beside = band_at(jnp.where(before_step, 1 - RING, RING - 1))
    ahead, behind = lat + RING < lat_size, lat >= RING
    relays_south = after_step & ahead
    relays_north = before_step & behind

    barrier = pltpu.get_barrier_semaphore()

    def greet(row):
        pl.semaphore_signal(barrier, inc=1, device_id=(row, lev), device_id_type=MESH)

    def peer(step):
        return lax.rem(lev + 1 + step, PEERS)

    pl.when(has_north)(lambda: greet(band_at(-1)))
    pl.when(has_south)(lambda: greet(band_at(1)))
    for step in range(PEERS - 1):
        pl.semaphore_signal(barrier, inc=1, device_id=(lat, peer(step)), device_id_type=MESH)
    guests = PEERS - 1 + jnp.where(has_north, 1, 0) + jnp.where(has_south, 1, 0)
    if relayed:

        @pl.when(before_step | after_step)
        def _():
            greet(beside)
            pl.when(ahead)(lambda: greet(band_at(RING)))
            pl.when(behind)(lambda: greet(band_at(-RING)))

        more = 1 + jnp.where(ahead, 1, 0) + jnp.where(behind, 1, 0)
        guests = guests + jnp.where(before_step | after_step, more, 0)

    sub = lax.broadcasted_iota(jnp.int32, (8, 128), 0)
    lanes_in = lax.broadcasted_iota(jnp.int32, (8, 128), 1)
    small = sub < 4

    for copy in own:
        copy.wait()

    def unpack(t):
        at = t * 128
        for start, n in ((0, 0), (LON, 64)):
            xs = [band[n + 8 * i : n + 8 * i + 8, pl.ds(at, 128)] for i in range(8)]
            for r, x in enumerate(transposed(xs)):
                rows[ROWS + r, :, pl.ds(start + at, 128)] = x
        xs = [jnp.log(band[128 + 8 * i : 136 + 8 * i, pl.ds(at, 128)]) for i in range(4)]
        for r, x in enumerate(transposed(xs + xs)):
            s_0[ROWS + r, :, pl.ds(at, 128)] = x

    for t in range(TILES):
        unpack(t)

    def fold(r, carry):
        j = ROWS + r
        for t in range(4):
            x = jnp.where(small, s_0[j, :, lane(t)], s_0[j, :, lane(t + 5)])
            rows[j, :, 2 * LON + 128 * t : 2 * LON + 128 * (t + 1)] = x
        rows[j, :, 2 * LON + 512 :] = s_0[j, :, lane(4)]
        return carry

    lax.fori_loop(0, ROWS, fold, 0)

    pl.semaphore_wait(barrier, guests)

    def remote(src, dst, send, recv, to):
        return pltpu.make_async_remote_copy(
            src_ref=src, dst_ref=dst, send_sem=send, recv_sem=recv, device_id=to, device_id_type=MESH
        )

    def to_south(h, src=None, row=None, send=None):
        return remote(
            rows.at[2 * ROWS - h] if src is None else src,
            rows.at[ROWS - h],
            halo_send.at[0, h - 1] if send is None else send,
            halo_recv.at[0, h - 1],
            (band_at(1) if row is None else row, lev),
        )

    def to_north(h, src=None, row=None, send=None):
        return remote(
            rows.at[ROWS - 1 + h] if src is None else src,
            rows.at[2 * ROWS - 1 + h],
            halo_send.at[1, h - 1] if send is None else send,
            halo_recv.at[1, h - 1],
            (band_at(-1) if row is None else row, lev),
        )

    def to_relay(way, h):
        n = RELAYED.index(h)
        src = rows.at[2 * ROWS - h] if way == 0 else rows.at[ROWS - 1 + h]
        return remote(src, relay.at[n], halo_send.at[way, h - 1], relay_recv.at[n], (beside, lev))

    for h in range(1, ROWS + 1):
        if relayed and h in RELAYED:
            pl.when(has_south & before_step)(lambda h=h: to_relay(0, h).start())
            pl.when(has_south & jnp.logical_not(before_step))(lambda h=h: to_south(h).start())
            pl.when(has_north & after_step)(lambda h=h: to_relay(1, h).start())
            pl.when(has_north & jnp.logical_not(after_step))(lambda h=h: to_north(h).start())
        else:
            pl.when(has_south)(lambda h=h: to_south(h).start())
            pl.when(has_north)(lambda h=h: to_north(h).start())

    def forward_south(h):
        return to_south(h, relay.at[RELAYED.index(h)], band_at(RING), relay_send.at[RELAYED.index(h)])

    def forward_north(h):
        return to_north(h, relay.at[RELAYED.index(h)], band_at(-RING), relay_send.at[RELAYED.index(h)])

    def pass_on(h):
        @pl.when(relays_south)
        def _():
            to_relay(0, h).wait_recv()
            forward_south(h).start()

        @pl.when(relays_north)
        def _():
            to_relay(1, h).wait_recv()
            forward_north(h).start()

    for copy in later:
        copy.wait()
    total = jnp.float32(0.0)
    for k in range(4 * PEERS):
        total = total + frac[k]
        share[k, :] = jnp.full((128,), frac[k], jnp.float32)
        bound[k, :] = jnp.full((128,), total, jnp.float32)
    share[...] = share[...] / total
    bound[...] = bound[...] / total
    bottoms[...] = jnp.zeros((8, 128), jnp.float32)
    bases[...] = jnp.zeros((PEERS, 8, 128), jnp.float32)
    row_of = lax.broadcasted_iota(jnp.int32, (3 * ROWS, 8, 128), 0) + (lat - 1) * ROWS
    angle = -0.5 * math.pi + (row_of.astype(jnp.float32) + 0.5) * (math.pi / (lat_size * ROWS))
    sign = jnp.where(lax.broadcasted_iota(jnp.int32, (3 * ROWS, 8, 128), 1) < 4, ROTATION_RATE, -ROTATION_RATE)
    turn[...] = sign * jnp.sin(angle)

    def inside(j):
        row = (lat - 1) * ROWS + j
        return jnp.where((row >= 0) & (row < lat_size * ROWS), 1.0, 0.0).astype(jnp.float32)

    def advance(state, js, emits):
        (uv_ref, _), (pq_ref, pq_at), (s_ref, _) = state
        fields = ((uv_ref, 0), (pq_ref, pq_at), (s_ref, 0))

        def line(j, emit):
            spin = turn[j]

            def load(n, row, t):
                ref, at = fields[n]
                return ref[row, :, at + 128 * t : at + 128 * (t + 1)]

            here, rolled = {}, {}

            def value(n, t):
                if (n, t) not in here:
                    here[n, t] = load(n, j, t)
                return here[n, t]

            def roll(n, t, k):
                t = t % TILES
                if (n, t, k) not in rolled:
                    rolled[n, t, k] = pltpu.roll(value(n, t), k, 1)
                return rolled[n, t, k]

            def east(n, t):
                one = jnp.where(lanes_in < 127, roll(n, t, 127), roll(n, t + 1, 127)) - jnp.where(
                    lanes_in < 1, roll(n, t - 1, 1), roll(n, t, 1)
                )
                two = jnp.where(lanes_in < 126, roll(n, t, 126), roll(n, t + 1, 126)) - jnp.where(
                    lanes_in < 2, roll(n, t - 1, 2), roll(n, t, 2)
                )
                return 8.0 * one - two

            def up(n, t):
                return 8.0 * (load(n, j + 1, t) - load(n, j - 1, t)) - (load(n, j + 2, t) - load(n, j - 2, t))

            def step(t):
                uv, pq, s = (value(n, t) for n in range(3))
                turned = flip(uv)
                eastward = jnp.where(small, uv, turned) * ADVECT
                northward = jnp.where(small, turned, uv) * ADVECT
                uv_east, uv_up = east(0, t), up(0, t)
                s_east, s_up = east(2, t), up(2, t)
                new_pq = pq - eastward * east(1, t) - northward * up(1, t)
                push = PRESS * jnp.where(small, s_east, s_up)
                new_uv = uv - eastward * uv_east - northward * uv_up - push + spin * turned
                spread = jnp.where(small, uv_east, uv_up)
                new_s = s - eastward * s_east - northward * s_up - ADVECT * (spread + flip(spread))
                emit(t, new_uv, new_pq, new_s)

            return step

        steps = [line(j, emit) for j, emit in zip(js, emits)]
        for t in range(TILES):
            for step in steps:
                step(t)

    states = (
        ((rows, 0), (rows, LON), (s_0, 0)),
        ((uv_1, 0), (pq_1, 0), (s_1, 0)),
        ((uv_2, 0), (pq_2, 0), (s_2, 0)),
        ((uv_3, 0), (pq_3, 0), (s_3, 0)),
    )

    def substep(n, *js):
        dst = states[n]

        def into(j):
            keep = inside(j)

            def emit(t, new_uv, new_pq, new_s):
                dst[0][0][j, :, lane(t)] = new_uv * keep
                dst[1][0][j, :, lane(t)] = new_pq
                dst[2][0][j, :, lane(t)] = new_s * keep

            return emit

        advance(states[n - 1], js, [into(j) for j in js])

    def receive(way, h):
        j = ROWS - h if way == 0 else 2 * ROWS - 1 + h
        there = has_north if way == 0 else has_south
        pl.when(there)(lambda: (to_south(h) if way == 0 else to_north(h)).wait_recv())

        @pl.when(jnp.logical_not(there))
        def _():
            rows[j] = jnp.zeros((8, ROW), jnp.float32)

        for t in range(5):
            x = rows[j, :, 2 * LON + 128 * t : 2 * LON + 128 * (t + 1)]
            y = flip(x)
            s_0[j, :, lane(t)] = jnp.where(small, x, y)
            if t < 4:
                s_0[j, :, lane(t + 5)] = jnp.where(small, y, x)

    def fwd_copy(q, step):
        to = peer(step)
        return remote(fwd.at[q, to], got.at[q, lev], fwd_send.at[q, step], fwd_recv.at[q, step], (lat, to))

    def extra_copy(q, side, to, step):
        dst = got.at[4, lev, :, pl.ds(0, PIECE)]
        return remote(extra.at[q, side], dst, fwd_send.at[4, step], fwd_recv.at[4, step], (lat, to))

    def release(q):
        pair = (3 - q, 4 + q)

        def into(side, r):
            at = side * PIECE

            def emit(t, new_uv, new_pq, new_s):
                if t < 8:
                    to = lax.rem(r + t, PEERS)
                    fwd[q, to, :, at : at + 128] = new_uv
                    fwd[q, to, :, at + 128 : at + 256] = new_pq
                    s_4[side, to] = new_s
                else:
                    extra[q, side, :, lane(0)] = new_uv
                    extra[q, side, :, lane(1)] = new_pq
                    extra[q, side, :, lane(2)] = new_s

            return emit

        advance(states[3], [ROWS + r for r in pair], [into(side, r) for side, r in enumerate(pair)])
        for to in range(PEERS):
            fwd[q, to, :, lane(2)] = jnp.where(small, s_4[0, to], s_4[1, to])
        lax.fori_loop(0, PEERS - 1, lambda k, z: (fwd_copy(q, k).start(), z)[1], 0)
        got[q, lev] = fwd[q, lev]
        for side, r in enumerate(pair):
            step = lax.rem(r - lev - 1 + 2 * PEERS, PEERS)
            pl.when(r != lev)(lambda side=side, r=r, step=step: extra_copy(q, side, r, step).start())

            @pl.when(r == lev)
            def _(side=side):
                got[4, lev, :, 0:PIECE] = extra[q, side]

    def ret_copy(q, step):
        to, lanes = peer(step), pl.ds(0, PAIR if q is None else 512)
        n = 4 if q is None else q
        dst = back.at[n, lev, :, lanes]
        return remote(ret.at[n, to, :, lanes], dst, ret_send.at[n, step], ret_recv.at[n, step], (lat, to))

    def own_copy(q):
        return pltpu.make_async_copy(ret.at[q, lev], back.at[q, lev], own_sem.at[q])

    def running(values):
        out, carry = [], None
        for v in values:
            for d in (1, 2, 4):
                v = v + jnp.where(sub >= d, pltpu.roll(v, d, 0), 0.0)
            if carry is not None:
                v = v + carry
            out.append(v)
            carry = v[7:8]
        return out

    def previous(values):
        out, carry = [], jnp.zeros((1, 128), jnp.float32)
        for v in values:
            out.append(jnp.where(sub == 0, carry, pltpu.roll(v, 1, 0)))
            carry = v[7:8]
        return out

    def gather(x, index):
        return jnp.take_along_axis(x, index, axis=0, mode="promise_in_bounds")

    def remap(q, side):
        first = side == 0
        row = jnp.where(q == 4, lev, jnp.where(first, 3 - q, 4 + q))
        t = jnp.where(q == 4, 8, lax.rem(lev - row + 2 * PEERS, PEERS))
        at, ret_at = side * PIECE, side * 256

        def split(n):
            xs = [got[q, p, :, pl.ds(pl.multiple_of(at + 128 * n, 128), 128)] for p in range(PEERS)]
            one = [jnp.where(small, xs[2 * i], flip(xs[2 * i + 1])) for i in range(4)]
            two = [jnp.where(small, flip(xs[2 * i]), xs[2 * i + 1]) for i in range(4)]
            return one, two

        zonal, meridional = split(0)
        temp, tracer = split(1)
        xs = [got[q, p, :, lane(2)] for p in range(PEERS)]
        layer = []
        for i in range(4):
            one = jnp.where(small, xs[2 * i], flip(xs[2 * i + 1]))
            two = jnp.where(small, flip(xs[2 * i]), xs[2 * i + 1])
            layer.append(jnp.exp(jnp.where(first, one, two)))
        lower = running(layer)
        upper = [x - y for x, y in zip(lower, layer)]
        bottom = lower[3][7:8]
        fields = (zonal, meridional, temp, tracer)
        before = []
        for f in fields:
            weighted = [x * y for x, y in zip(f, layer)]
            before.append([x - y for x, y in zip(running(weighted), weighted)])
        target = [bottom * bound[8 * i : 8 * i + 8, :] for i in range(4)]
        integral = [[] for _ in fields]
        ends = [lower[m][7:8] for m in range(3)]
        mids = [jnp.broadcast_to(lower[m][3:4], (8, 128)) for m in range(4)]
        for i in range(4):
            goal = target[i]
            past = [goal > e for e in ends]

            def pick(x):
                return jnp.where(past[2], x[3], jnp.where(past[1], x[2], jnp.where(past[0], x[1], x[0])))

            pos = jnp.where(pick(mids) < goal, 4, 0)
            pos = pos + jnp.where(pick([gather(x, pos + 1) for x in lower]) < goal, 2, 0)
            pos = pos + jnp.where(pick([gather(x, pos) for x in lower]) < goal, 1, 0)

            def here(xs):
                return pick([gather(x, pos) for x in xs])

            depth = goal - here(upper)
            for n, f in enumerate(fields):
                integral[n].append(here(before[n]) + depth * here(f))
        new_thick = [bottom * share[8 * i : 8 * i + 8, :] for i in range(4)]
        inverse = [1.0 / x for x in new_thick]
        remapped = [[(x - y) * z for x, y, z in zip(g, previous(g), inverse)] for g in integral]
        rise = [
            r * jnp.log((TOP_PRESSURE + x) / (TOP_PRESSURE + y))
            for r, x, y in zip(remapped[2], target, previous(target))
        ]
        geo = [None] * 4
        ground = surf[:, pl.ds(pl.multiple_of(t * 128, 128), 128)]
        ground_row = jnp.sum(jnp.where(sub == row, ground, 0.0), axis=0, keepdims=True)
        carry = ground_row
        for i in (3, 2, 1, 0):
            x = rise[i]
            for d in (1, 2, 4):
                x = x + jnp.where(sub < 8 - d, pltpu.roll(x, 8 - d, 0), 0.0)
            geo[i] = x + carry
            carry = geo[i][0:1]
        for n, (one, two) in enumerate(((remapped[0], remapped[1]), (remapped[2], remapped[3]))):
            lanes = pl.ds(pl.multiple_of(ret_at + 128 * n, 128), 128)
            for i in range(4):
                ret[q, 2 * i, :, lanes] = jnp.where(small, one[i], flip(two[i]))
                ret[q, 2 * i + 1, :, lanes] = jnp.where(small, flip(one[i]), two[i])
        floor = jnp.broadcast_to(bottom, (8, 128))
        below = [x for i in range(4) for x in (geo[i][4:5], geo[i + 1][0:1] if i < 3 else ground_row)]

        @pl.when(q < 4)
        def _():
            bottoms[...] = jnp.where(sub == row, floor, bottoms[...])
            for p in range(PEERS):
                bases[p] = jnp.where(sub == row, below[p], bases[p])

        @pl.when(q == 4)
        def _():
            for p in range(PEERS):
                ret[4, p, :, lane(2)] = jnp.where(small, floor, below[p])
                ret[4, p, :, lane(3)] = bottoms[...]
                ret[4, p, :, lane(4)] = bases[p]

    def process(q):
        lax.fori_loop(0, PEERS - 1, lambda k, z: (fwd_copy(q, k).wait_recv(), z)[1], 0)
        lax.fori_loop(0, 2, lambda side, z: (remap(q, side), z)[1], 0)
        lax.fori_loop(0, PEERS - 1, lambda k, z: (ret_copy(q, k).start(), z)[1], 0)
        own_copy(q).start()

    lax.fori_loop(5, 7, lambda m, z: (substep(1, 2 * m, 2 * m + 1), z)[1], 0)

    def front(h, depth):
        receive(0, h)
        receive(1, h)
        for n in range(1, min(depth, 3) + 1):
            substep(n, 8 + 2 * n - h, 15 - 2 * n + h)
        if depth == 4:
            release(h - 5)

    def passing(h):
        if relayed:
            pass_on(h)

    def late(m, carry):
        front(5 + 2 * m, 4)
        pl.when(m == 1)(lambda: process(0))
        front(6 + 2 * m, 4)
        pl.when(m == 1)(lambda: process(1))
        return carry

    passing(3)
    front(1, 2)
    passing(5)
    front(2, 2)
    passing(7)
    front(3, 3)
    front(4, 3)
    lax.fori_loop(0, 2, late, 0)
    lax.fori_loop(2, 4, lambda q, z: (process(q), z)[1], 0)
    lax.fori_loop(0, PEERS - 1, lambda k, z: (extra_copy(0, 0, 0, k).wait_recv(), z)[1], 0)
    remap(4, 0)
    lax.fori_loop(0, PEERS - 1, lambda k, z: (ret_copy(None, k).start(), z)[1], 0)
    own_copy(4).start()
    for q in (0, 1, 2, 3, None):
        lax.fori_loop(0, PEERS - 1, lambda k, z, q=q: (ret_copy(q, k).wait(), z)[1], 0)
    for q in range(5):
        own_copy(q).wait()
    for q in range(4):
        lax.fori_loop(0, PEERS - 1, lambda k, z, q=q: (fwd_copy(q, k).wait_send(), z)[1], 0)
    lax.fori_loop(0, PEERS - 1, lambda k, z: (extra_copy(0, 0, 0, k).wait_send(), z)[1], 0)
    for h in range(1, ROWS + 1):
        pl.when(has_south)(lambda h=h: to_south(h).wait_send())
        pl.when(has_north)(lambda h=h: to_north(h).wait_send())
    if relayed:
        for h in RELAYED:
            pl.when(relays_south)(lambda h=h: forward_south(h).wait_send())
            pl.when(relays_north)(lambda h=h: forward_north(h).wait_send())


def publish(back, frac_ref, out_ref, out_thick_ref, out_geo_ref, frac, held, out, thick, heights, read_sem, write_sem):
    lev = lax.axis_index("lev")
    fractions = pltpu.make_async_copy(frac_ref, frac, read_sem.at[5])
    fractions.start()
    reads = [pltpu.make_async_copy(back.at[n], held.at[n], read_sem.at[n]) for n in range(5)]
    for copy in reads:
        copy.start()
    fractions.wait()

    total, above = jnp.float32(0.0), [jnp.float32(0.0)] * 5
    for k in range(4 * PEERS):
        for i in range(5):
            above[i] = jnp.where(k == 4 * lev + i, total, above[i])
        total = total + frac[k]
    above[4] = jnp.where(lev == PEERS - 1, total, above[4])
    bounds = [jnp.full((8, 128), x, jnp.float32) / total for x in above]
    shares = [jnp.full((8, 128), frac[4 * lev + i], jnp.float32) / total for i in range(4)]
    sub = lax.broadcasted_iota(jnp.int32, (8, 128), 0)

    def lane(t):
        return slice(128 * t, 128 * t + 128)

    def put(t, uv, pq, bottom, base):
        lanes = lane(t)
        uv, pq = transposed(uv), transposed(pq)
        for i in range(8):
            out[8 * i : 8 * i + 8, lanes] = uv[i]
            out[64 + 8 * i : 72 + 8 * i, lanes] = pq[i]
        pressure = [TOP_PRESSURE + bottom * x for x in bounds]
        height = base
        for i in (3, 2, 1, 0):
            height = height + pq[i] * jnp.log(pressure[i + 1] / pressure[i])
            heights[8 * i : 8 * i + 8, lanes] = height
            thick[8 * i : 8 * i + 8, lanes] = bottom * shares[i]

    def deliver(t):
        uv, pq = [], []
        bottom = base = jnp.zeros((8, 128), jnp.float32)
        for r in range(ROWS):
            owner, q, side = (r + t) % PEERS, max(3 - r, r - 4), r // 4
            uv.append(held[q, owner, :, lane(2 * side)])
            pq.append(held[q, owner, :, lane(2 * side + 1)])
            bottom = jnp.where(sub == r, held[4, owner, :, lane(3)], bottom)
            base = jnp.where(sub == r, held[4, owner, :, lane(4)], base)
        put(t, uv, pq, bottom, base)

    def deliver_last():
        bottom = base = jnp.zeros((8, 128), jnp.float32)
        for r in range(ROWS):
            x = held[4, r, :, lane(2)]
            bottom = jnp.where(sub == r, flip(x) if r >= 4 else x, bottom)
            base = jnp.where(sub == r, x if r >= 4 else flip(x), base)
        put(8, [held[4, r, :, lane(0)] for r in range(ROWS)], [held[4, r, :, lane(1)] for r in range(ROWS)], bottom, base)

    for copy in reads:
        copy.wait()
    writes = []
    for c in range(3):
        for t in range(3 * c, min(3 * c + 3, TILES - 1)):
            deliver(t)
        if c == 2:
            deliver_last()
        lanes = pl.ds(384 * c, 384)
        for n, (src, dst) in enumerate(((out, out_ref), (thick, out_thick_ref), (heights, out_geo_ref))):
            writes.append(pltpu.make_async_copy(src.at[:, lanes], dst.at[:, lanes], write_sem.at[c, n]))
            writes[-1].start()
    for copy in writes:
        copy.wait()


def shards(lat_size, velocity, potential_temp, tracer, thickness, surface_height, level_fractions):
    hbm = pl.BlockSpec(memory_space=pltpu.HBM)
    f32 = jnp.float32
    out_shape = (
        jax.ShapeDtypeStruct((128, LON), f32),
        jax.ShapeDtypeStruct((32, LON), f32),
        jax.ShapeDtypeStruct((32, LON), f32),
    )
    returned = pl.pallas_call(
        functools.partial(kernel, lat_size),
        out_shape=jax.ShapeDtypeStruct((5, PEERS, 8, PAIR), f32),
        in_specs=[hbm] * 6,
        out_specs=hbm,
        scratch_shapes=[
            pltpu.SMEM((32,), f32),
            pltpu.VMEM((160, LON), f32),
            pltpu.VMEM((3 * ROWS, 8, ROW), f32),
            *[pltpu.VMEM((3 * ROWS, 8, LON), f32)] * 10,
            pltpu.VMEM((3 * ROWS, 8, 128), f32),
            pltpu.VMEM((32, 128), f32),
            pltpu.VMEM((32, 128), f32),
            pltpu.VMEM((ROWS, LON), f32),
            pltpu.VMEM((len(RELAYED), 8, ROW), f32),
            pltpu.VMEM((4, PEERS, 8, PAIR), f32),
            pltpu.VMEM((4, 2, 8, PIECE), f32),
            pltpu.VMEM((2, PEERS, 8, 128), f32),
            pltpu.VMEM((5, PEERS, 8, PAIR), f32),
            pltpu.VMEM((5, PEERS, 8, PAIR), f32),
            pltpu.VMEM((8, 128), f32),
            pltpu.VMEM((PEERS, 8, 128), f32),
            pltpu.SemaphoreType.DMA((6,)),
            pltpu.SemaphoreType.DMA((2, ROWS)),
            pltpu.SemaphoreType.DMA((2, ROWS)),
            pltpu.SemaphoreType.DMA((len(RELAYED),)),
            pltpu.SemaphoreType.DMA((len(RELAYED),)),
            pltpu.SemaphoreType.DMA((5, PEERS - 1)),
            pltpu.SemaphoreType.DMA((5, PEERS - 1)),
            pltpu.SemaphoreType.DMA((5, PEERS - 1)),
            pltpu.SemaphoreType.DMA((5, PEERS - 1)),
            pltpu.SemaphoreType.DMA((5,)),
        ],
        compiler_params=pltpu.CompilerParams(
            collective_id=0, has_side_effects=True, vmem_limit_bytes=60 * 2**20
        ),
        cost_estimate=pl.CostEstimate(flops=10**8, bytes_accessed=2 * 10**6, transcendentals=10**6),
    )(
        velocity.reshape(64, LON),
        potential_temp.reshape(32, LON),
        tracer.reshape(32, LON),
        thickness.reshape(32, LON),
        surface_height,
        level_fractions,
    )
    remapped, new_thickness, geopotential = pl.pallas_call(
        publish,
        out_shape=out_shape,
        in_specs=[hbm] * 2,
        out_specs=(hbm,) * 3,
        scratch_shapes=[
            pltpu.SMEM((32,), f32),
            pltpu.VMEM((5, PEERS, 8, PAIR), f32),
            pltpu.VMEM((128, LON), f32),
            pltpu.VMEM((32, LON), f32),
            pltpu.VMEM((32, LON), f32),
            pltpu.SemaphoreType.DMA((6,)),
            pltpu.SemaphoreType.DMA((3, 3)),
        ],
        compiler_params=pltpu.CompilerParams(vmem_limit_bytes=60 * 2**20),
        cost_estimate=pl.CostEstimate(flops=0, bytes_accessed=2 * 10**6, transcendentals=0),
    )(returned, level_fractions)
    return (
        remapped.reshape(4, 4, ROWS, LON),
        new_thickness.reshape(4, ROWS, LON),
        geopotential.reshape(4, ROWS, LON),
    )


def solution(mesh):
    return jax.shard_map(
        functools.partial(shards, mesh.shape["lat"]),
        mesh=mesh,
        in_specs=(
            P(None, "lev", "lat", None),
            P("lev", "lat", None),
            P("lev", "lat", None),
            P("lev", "lat", None),
            P("lat", None),
            P(),
        ),
        out_specs=(P(None, "lev", "lat", None), P("lev", "lat", None), P("lev", "lat", None)),
        check_vma=False,
    )
```
